256 devices in a mesh: seq: 16 (over z_lo, x), dp: 16 (over z_hi, y, core).
Axes of the slice: x: 4, y: 4, z: 8 (z_hi: 2, z_lo: 4; z = z_hi * 4 + z_lo), core: 2. Of those that a mesh axis runs over, the one named last changes fastest.
Arguments:
- bases: int32 [65536], P(('dp', 'seq')), parts along dimension 0, may hold values from 0 to 3
- targets: int32 [16384, 128], P(('dp', 'seq')), parts along dimension 0, may hold values from 0 to 4
- w_conv: float32 [60, 768], replicated, may hold values from -1.5 to 1.5
- w_query: float32 [768, 512], replicated, may hold values from -12.5 to 12.5
- w_key: float32 [768, 512], replicated, may hold values from -0.31 to 0.31
- w_value: float32 [768, 512], replicated, may hold values from -0.21875 to 0.21875
- w_out: float32 [512, 768], replicated, may hold values from -0.25 to 0.25
- w_head: float32 [768, 128], replicated, may hold values from -0.21875 to 0.21875
Outputs:
- log_rate: float32 [16384, 128], P(('dp', 'seq')), parts along dimension 0
- d_conv: float32 [960, 768], P('dp', 'seq'), parts along dimension 0
- d_query: float32 [12288, 512], P(('dp', 'seq')), parts along dimension 0
- d_key: float32 [12288, 512], P(('dp', 'seq')), parts along dimension 0
- d_value: float32 [12288, 512], P(('dp', 'seq')), parts along dimension 0
- d_out: float32 [8192, 768], P(('dp', 'seq')), parts along dimension 0
- d_head: float32 [12288, 128], P(('dp', 'seq')), parts along dimension 0
The draws below stay inside these ranges and needn't reach their ends.
There are 16 independent parts, one for each index of `dp`. The reference program is written for one: setup_inputs(seed, part) draws one part's arguments, and reference() takes and returns one part's arrays. A program takes and returns all parts, laid end to end along the dimension named above; an argument that names none is the same for every part. Nothing has to cross between parts.
All inputs are finite; a program needn't handle non-finite values.
Results may differ from the reference program's by a relative error of at most 0.0003.
Values sent between devices are 32-bit elements; how exact they have to be, the bound alone decides.
No kernel may reach another device: no remote copies, remote signals or barrier semaphores. Data moves between devices by JAX's collectives and lax.ppermute only.
A program may use at most 128 MiB of HBM per device.

```python
import math
import jax
import jax.numpy as jnp
from jax import lax

C = 768
KW = 15
HEADS = 8
HS = 64
TRACKS = 128
POOL = 4
HD = 512
TOKENS = 1024
SEQ_BP = 4096


def shared_base(key):
    return jax.random.uniform(key, (C, HD), jnp.float32, -1.7320508, 1.7320508)


def draw_w_key(key, part):
    base = shared_base(key)
    return base * C ** (-0.5)


def draw_w_query(key, part):
    key = jax.random.fold_in(key, 5)
    fresh = jax.random.uniform(key, (C, HD), jnp.float32, -1.7320508, 1.7320508)
    return fresh * C ** (-0.5)


def set_ends(array, own_key, smallest, top_value):
    place = [jax.random.randint(jax.random.fold_in(own_key, axis), (), 0, length) for axis, length in enumerate(array.shape)]
    longest = array.shape.index(max(array.shape))
    beside = place[:longest] + [(place[longest] + 1) % array.shape[longest]] + place[longest + 1:]
    return array.at[tuple(place)].set(smallest).at[tuple(beside)].set(top_value)


def gaussian(own_key, extent, width, most, kind=jnp.bfloat16):
    array = width * jax.random.normal(own_key, extent, jnp.float32)
    return jnp.clip(array, min=-most, max=most).astype(kind)


def setup_inputs(seed: int = 0, part: int = 0) -> dict:
    splits = jax.random.split(jax.random.key(seed), 9)
    own_keys = jax.random.split(jax.random.fold_in(splits[8], part), 9)
    bases = set_ends(jax.random.randint(own_keys[0], (SEQ_BP,), 0, 4), jax.random.fold_in(own_keys[0], 1), 0, 3).astype(jnp.int32)
    targets = set_ends(jax.random.randint(own_keys[1], (TOKENS, TRACKS), 0, 5), jax.random.fold_in(own_keys[1], 1), 0, 4).astype(jnp.int32)
    w_conv = gaussian(splits[2], (4 * KW, C), KW ** -0.5, 1.5, jnp.float32)
    w_query = draw_w_query(jax.random.fold_in(splits[8], 71), part)
    w_key = draw_w_key(jax.random.fold_in(splits[8], 71), part)
    w_value = gaussian(splits[5], (C, HD), C ** -0.5, 0.21875, jnp.float32)
    w_out = gaussian(splits[6], (HD, C), HD ** -0.5, 0.25, jnp.float32)
    w_head = gaussian(splits[7], (C, TRACKS), C ** -0.5, 0.21875, jnp.float32)
    return {"bases": bases, "targets": targets, "w_conv": w_conv, "w_query": w_query, "w_key": w_key, "w_value": w_value, "w_out": w_out, "w_head": w_head}


def matmul(left, right):
    return jnp.dot(left, right, precision=lax.Precision.HIGHEST)

def rms_norm(values):
    return values * lax.rsqrt(lax.optimization_barrier(jnp.mean(values * values, axis=-1, keepdims=True)) + 1e-06)

def one_head(triple):
    queries, keys_one, values_one = triple
    scores = matmul(queries, keys_one.T) * HS ** (-0.5)
    return matmul(jax.nn.softmax(scores, axis=-1), values_one)

def forward(w_conv, w_query, w_key, w_value, w_out, w_head, columns):
    hidden = jax.nn.gelu(matmul(columns, w_conv))
    pooled = hidden.reshape(TOKENS, POOL, C).mean(axis=1)
    normed = rms_norm(pooled)
    split_q = matmul(normed, w_query).reshape(TOKENS, HEADS, HS).transpose(1, 0, 2)
    split_k = matmul(normed, w_key).reshape(TOKENS, HEADS, HS).transpose(1, 0, 2)
    split_v = matmul(normed, w_value).reshape(TOKENS, HEADS, HS).transpose(1, 0, 2)
    attended = lax.map(one_head, (split_q, split_k, split_v)).transpose(1, 0, 2).reshape(TOKENS, HD)
    summed = pooled + matmul(attended, w_out)
    return matmul(rms_norm(summed), w_head)

def reference(bases, targets, w_conv, w_query, w_key, w_value, w_out, w_head):
    onehot = jax.nn.one_hot(bases, 4, dtype=jnp.float32)
    padded = jnp.pad(onehot, ((KW // 2, KW // 2), (0, 0)))
    columns = jnp.concatenate([padded[j:j + SEQ_BP] for j in range(KW)], axis=1)

    def apply_weights(wc, wq, wk, wv, wo, wh):
        return forward(wc, wq, wk, wv, wo, wh, columns)
    log_rate, pullback = jax.vjp(apply_weights, w_conv, w_query, w_key, w_value, w_out, w_head)
    grad_rate = (jnp.exp(log_rate) - targets.astype(jnp.float32)) / math.sqrt(TOKENS)
    d_conv, d_query, d_key, d_value, d_out, d_head = pullback(grad_rate)
    return (log_rate, d_conv, d_query, d_key, d_value, d_out, d_head)
```

```python
import math

import jax
import jax.numpy as jnp
from jax import lax
from jax.experimental import pallas as pl
from jax.experimental.pallas import tpu as pltpu
from jax.sharding import PartitionSpec as P


C = 768
KW = 15
HEADS = 8
HS = 64
TRACKS = 128
POOL = 4
HD = 512
TOKENS = 1024
GROUP = 8
OWN = 64
F32 = jnp.float32
BF16 = jnp.bfloat16
GELU_A = math.sqrt(2.0 / math.pi)
GELU_B = GELU_A * 0.044715
WIN = 80
TILE = 256

VMEM = pl.BlockSpec(memory_space=pltpu.VMEM)
SMEM = pl.BlockSpec(memory_space=pltpu.SMEM)
ANY = pl.BlockSpec(memory_space=pl.ANY)


def dot(left, right):
    return lax.dot_general(left, right, (((1,), (0,)), ((), ())), preferred_element_type=F32)


def split2(a):
    hi = a.astype(BF16)
    return hi, (a - hi.astype(F32)).astype(BF16)


def split3(a):
    hi = a.astype(BF16)
    rest = a - hi.astype(F32)
    mid = rest.astype(BF16)
    return hi, mid, (rest - mid.astype(F32)).astype(BF16)


def dot3(left, right):
    lh, ll = split2(left)
    rh, rl = split2(right)
    return dot(lh, rh) + (dot(lh, rl) + dot(ll, rh))


def dot3_narrow(left, right):
    lh, ll = split2(left)
    rh, rl = split2(right)
    n = right.shape[1]
    both = dot(lh, jnp.concatenate([rh, rl], axis=1))
    return both[:, :n] + (both[:, n:] + dot(ll, rh))


def dot3_short(left, right):
    lh, ll = split2(left)
    rh, rl = split2(right)
    n = left.shape[0]
    both = dot(jnp.concatenate([lh, ll], axis=0), rh)
    return both[:n] + (both[n:] + dot(lh, rl))


def dot3_thin(left, right):
    lh, ll = split2(left)
    rh, rl = split2(right)
    return dot(jnp.concatenate([lh, lh, ll], axis=1), jnp.concatenate([rh, rl, rh], axis=0))


def dot6(left, right):
    lh, lm, ll = split3(left)
    rh, rm, rl = split3(right)
    return dot(lh, rh) + ((dot(lh, rm) + dot(lm, rh)) + (dot(lm, rm) + (dot(lh, rl) + dot(ll, rh))))


def rms_scale(a):
    return lax.rsqrt(jnp.mean(a * a, axis=-1, keepdims=True) + 1e-06)


def conv_weights(w_ref, pad_ref, out_ref):
    pad_ref[...] = jnp.zeros_like(pad_ref)
    for r in range(POOL):
        pad_ref[r, 4 * (r + 1):4 * (r + 1) + 4 * KW, :] = w_ref[...]
    for r in range(POOL):
        pieces = split3(pad_ref[r])
        zeros = jnp.zeros((256 - 3 * WIN, C), BF16)
        out_ref[:, r * C:(r + 1) * C] = jnp.concatenate([*pieces, zeros], axis=0)


def key_stack(k):
    h, m, l = split3(k)
    return jnp.concatenate([h, m, l, h, m, h], axis=1)


def query_stack(q_t):
    h, m, l = split3(q_t)
    return jnp.concatenate([h, h, h, m, m, l], axis=0)


def attend_kernel(
    info, bases, w_conv, wq_hbm, wk_hbm, wv_hbm,
    xh_out, xl_out, x_own, hot_own, qkv_out, o_out,
    pad, w_all, window, slabs, x_all, hot_all, sems,
):
    half, m = info[0], info[1]
    copies = []
    for i, w in enumerate((wq_hbm, wk_hbm, wv_hbm)):
        lanes = pl.ds(pl.multiple_of(lax.div(m, 2) * 128, 128), 128)
        copies.append(pltpu.make_async_copy(w.at[:, lanes], slabs.at[i], sems.at[i]))
    for copy in copies:
        copy.start()
    conv_weights(w_conv, pad, w_all)

    lane = lax.broadcasted_iota(jnp.int32, (128, 256), 1)
    row = lax.broadcasted_iota(jnp.int32, (128, 256), 0)
    within = lax.rem(lane, WIN)
    place = lax.div(lax.rem(within, 16), 4)
    pick = jnp.where(lax.rem(row, 4) == place, 1.0, 0.0).astype(BF16)
    mine = lax.broadcasted_iota(jnp.int32, (32, 128), 0) == lax.div(lax.broadcasted_iota(jnp.int32, (32, 128), 1), 4)
    code = lax.rem(lax.broadcasted_iota(jnp.int32, (1, 256), 1), 4).astype(F32)
    window[0:8, :] = jnp.zeros((8, 256), F32)
    window[TOKENS + 8:TOKENS + 16, :] = jnp.zeros((8, 256), F32)
    for part in range(8):
        pieces = []
        for q in range(4 * part, 4 * part + 4):
            line = bases[q // 2, q % 2:q % 2 + 1, :].astype(F32)
            pieces.append(jnp.where(mine, jnp.broadcast_to(line, (32, 128)), 0.0))
        value = dot(jnp.concatenate(pieces, axis=0).astype(BF16), pick)
        window[8 + 128 * part:8 + 128 * part + 128, :] = jnp.where(value == code, 1.0, 0.0)

    shift = lax.div(lax.rem(lax.broadcasted_iota(jnp.int32, (TILE, 256), 1), WIN), 16)
    real = lax.broadcasted_iota(jnp.int32, (TILE, 256), 1) < 3 * WIN
    steps = TOKENS // TILE

    def encode(c, _):
        start = pl.multiple_of(lax.rem(c + half * (steps // 2), steps) * TILE, TILE)
        around = window[pl.ds(start, TILE + 16), :]
        hot = jnp.zeros((TILE, 256), F32)
        for d in range(5):
            hot = jnp.where(shift == d, around[6 + d:6 + d + TILE, :], hot)
        hot = jnp.where(real, hot, 0.0).astype(BF16)
        total = jnp.zeros((TILE, C), F32)
        for r in range(POOL):
            pre = dot(hot, w_all[:, r * C:(r + 1) * C])
            total += 0.5 * pre * (1.0 + jnp.tanh(pre * (GELU_A + GELU_B * (pre * pre))))
        x = total * (1.0 / POOL)
        here = pl.ds(pl.multiple_of(c * TILE, TILE), TILE)
        x_all[here, :] = x
        hot_all[here, :] = hot
        return 0

    lax.fori_loop(0, steps, encode, 0)
    for copy in copies:
        copy.wait()
    odd = lax.rem(m, 2) == 1
    w_qkv = jnp.concatenate([jnp.where(odd, slabs[i, :, HS:], slabs[i, :, :HS]) * (HS ** -0.5 if i == 0 else 1.0) for i in range(3)], axis=1)
    wh, wm, wl = split3(w_qkv)

    def project(c, _):
        here = pl.ds(pl.multiple_of(c * TILE, TILE), TILE)
        x = x_all[here, :]
        xn = x * rms_scale(x)
        h, mid, low = split3(xn)
        xh_out[here, :] = h
        xl_out[here, :] = mid
        qkv_out[here, :] = dot(h, wh) + ((dot(h, wm) + dot(mid, wh)) + (dot(mid, wm) + (dot(h, wl) + dot(low, wh))))
        return 0

    lax.fori_loop(0, steps, project, 0)
    for part in range(2):
        here = pl.ds(pl.multiple_of(part * 512 + m * OWN, OWN), OWN)
        x_own[part * OWN:(part + 1) * OWN, :] = x_all[here, :]
        hot_own[part * OWN:(part + 1) * OWN, :] = hot_all[here, :]

    qkv = qkv_out[...]
    q_t = query_stack(jnp.transpose(qkv[:, :HS]))
    keys = key_stack(qkv[:, HS:2 * HS])
    vh, vl = split2(jnp.transpose(qkv[:, 2 * HS:]))
    v_both = jnp.concatenate([vh, vl], axis=0)
    outs = []
    for c in range(steps):
        scores = dot(keys, q_t[:, c * TILE:(c + 1) * TILE])
        e = jnp.exp(scores - jnp.max(scores, axis=0, keepdims=True))
        total = jnp.sum(e, axis=0, keepdims=True)
        eh, el = split2(e)
        both = dot(v_both, eh)
        outs.append(jnp.transpose((both[:HS] + (both[HS:] + dot(vh, el))) / total))
    o_out[...] = jnp.concatenate(
        [jnp.concatenate(outs[:steps // 2], axis=0), jnp.concatenate(outs[steps // 2:], axis=0)], axis=1
    )


def decode_kernel(
    info, o_parts, x_own, targets_here, targets_there, w_out, w_head,
    log_rate, do_out, dy_out, grads_out, yn_all,
):
    half = info[0]
    parts = [o_parts[h * OWN:(h + 1) * OWN, :] for h in range(HEADS)]
    attended = jnp.concatenate(
        [jnp.concatenate([p[:, :HS] for p in parts], axis=1), jnp.concatenate([p[:, HS:] for p in parts], axis=1)], axis=0
    )
    wout = w_out[...]
    wouth, woutl = split2(wout)
    ah, al = split2(attended)
    both = dot(jnp.concatenate([ah, al], axis=0), wouth)
    y = x_own[...] + (both[:2 * OWN] + (both[2 * OWN:] + dot(ah, woutl)))
    scale = rms_scale(y)
    yn = y * scale
    yn_all[...] = yn
    rate = dot3_narrow(yn, w_head[...])
    log_rate[...] = rate[:OWN]
    targets = jnp.concatenate([targets_here[...], targets_there[...]], axis=0).astype(F32)
    d_rate = (jnp.exp(rate) - targets) * (1.0 / math.sqrt(TOKENS))
    d_yn = dot3_thin(d_rate, jnp.transpose(w_head[...]))
    dy = scale * (d_yn - yn * jnp.mean(d_yn * yn, axis=-1, keepdims=True))
    dy_out[...] = dy
    dth, dtl = split2(jnp.transpose(dy))
    both = dot(wouth, jnp.concatenate([dth, dtl], axis=1))
    do_out[...] = both[:, :2 * OWN] + (both[:, 2 * OWN:] + dot(woutl, dth))

    heads = o_parts[pl.ds(pl.multiple_of(half * 256, 256), 256), :]
    o_t = jnp.concatenate(
        [
            jnp.concatenate(
                [jnp.transpose(heads[h * OWN:(h + 1) * OWN, :])[:HS], jnp.transpose(heads[h * OWN:(h + 1) * OWN, :])[HS:]], axis=1
            )
            for h in range(4)
        ],
        axis=0,
    )
    d_out = dot3_thin(o_t, dy)
    yn_half = yn_all[:, pl.ds(pl.multiple_of(half * 384, 128), 384)]
    d_head = dot3_thin(jnp.transpose(yn_half), d_rate)
    for p in range(GROUP):
        for j in range(6):
            grads_out[p * 240 + 32 * j:p * 240 + 32 * j + 32, :] = d_out[32 * p:32 * p + 32, 128 * j:128 * j + 128]
        grads_out[p * 240 + 192:p * 240 + 240, :] = d_head[48 * p:48 * p + 48, :]


def attend_back_kernel(info, do_parts, qkv_ref, xh_hbm, xl_hbm, sent, xh, xl, do_all, g_t, dk_acc, dv_acc, sems):
    half = info[0]
    lanes = pl.ds(pl.multiple_of(half * 384, 128), 384)
    copies = [
        pltpu.make_async_copy(xh_hbm.at[:, lanes], xh, sems.at[0]),
        pltpu.make_async_copy(xl_hbm.at[:, lanes], xl, sems.at[1]),
    ]
    for copy in copies:
        copy.start()
    for p in range(GROUP):
        both = jnp.transpose(do_parts[p * OWN:(p + 1) * OWN, :])
        do_all[p * OWN:(p + 1) * OWN, :] = both[:OWN]
        do_all[512 + p * OWN:512 + (p + 1) * OWN, :] = both[OWN:]
    qkv = qkv_ref[...]
    q = qkv[:, :HS]
    k = qkv[:, HS:2 * HS]
    v = qkv[:, 2 * HS:]
    q_t = query_stack(jnp.transpose(q))
    keys = key_stack(k)
    kh, kl = split2(jnp.transpose(k))
    k_both = jnp.concatenate([kh, kl], axis=0)
    vh, vl = split2(v)
    v_three = jnp.concatenate([vh, vh, vl], axis=1)
    do = do_all[...]
    dth, dtl = split2(jnp.transpose(do))
    do_t = jnp.concatenate([dth, dtl, dth], axis=0)
    dh, dl = split2(do)
    do_both = jnp.concatenate([dh, dl], axis=1)
    qh, ql = split2(q)
    q_both = jnp.concatenate([qh, ql], axis=1)
    for c in range(TOKENS // TILE):
        here = slice(c * TILE, (c + 1) * TILE)
        scores = dot(keys, q_t[:, here])
        e = jnp.exp(scores - jnp.max(scores, axis=0, keepdims=True))
        p = e * (1.0 / jnp.sum(e, axis=0, keepdims=True))
        dp = dot(v_three, do_t[:, here])
        ds = p * (dp - jnp.sum(p * dp, axis=0, keepdims=True))
        ph, plow = split2(p)
        sh, sl = split2(ds)
        both = dot(k_both, sh)
        g_t[0:HS, here] = (both[:HS] + (both[HS:] + dot(kh, sl))) * (HS ** -0.5)
        both = dot(ph, do_both[here])
        dv = both[:, :HS] + (both[:, HS:] + dot(plow, dh[here]))
        both = dot(sh, q_both[here])
        dk = both[:, :HS] + (both[:, HS:] + dot(sl, qh[here]))
        if c == 0:
            dk_acc[...] = dk
            dv_acc[...] = dv
        else:
            dk_acc[...] += dk
            dv_acc[...] += dv
    g_t[HS:2 * HS, :] = jnp.transpose(dk_acc[...])
    g_t[2 * HS:3 * HS, :] = jnp.transpose(dv_acc[...])
    for p in range(GROUP):
        sent[p * 264:p * 264 + 192, :] = jnp.concatenate(
            [g_t[:, p * OWN:(p + 1) * OWN], g_t[:, 512 + p * OWN:512 + (p + 1) * OWN]], axis=1
        )
    for copy in copies:
        copy.wait()
    gh, gl = split2(g_t[...])
    both = dot(jnp.concatenate([gh, gl], axis=0), xh[...])
    d_w = jnp.transpose(both[:192] + (both[192:] + dot(gh, xl[...])))
    for p in range(GROUP):
        mine = d_w[48 * p:48 * p + 48, :]
        sent[p * 264 + 192:p * 264 + 240, :] = mine[:, :128]
        sent[p * 264 + 240:p * 264 + 264, :] = jnp.concatenate([mine[:24, 128:], mine[24:, 128:]], axis=1)


def encode_back_kernel(
    info, got, wq_hbm, wk_hbm, wv_hbm, w_conv, x_own, hot_own, dy,
    d_query, d_key, d_value, sent,
    pad, w_all, weights, slopes, dconv, sems,
):
    half = info[0]
    copies = [pltpu.make_async_copy(w, weights.at[i], sems.at[i]) for i, w in enumerate((wq_hbm, wk_hbm, wv_hbm))]
    for copy in copies:
        copy.start()
    conv_weights(w_conv, pad, w_all)
    hot = hot_own[...]
    for r in range(POOL):
        pre = dot(hot, w_all[:, r * C:(r + 1) * C])
        square = pre * pre
        t = jnp.tanh(pre * (GELU_A + GELU_B * square))
        slopes[:, r * C:(r + 1) * C] = 0.5 * (1.0 + t) + 0.5 * pre * (1.0 - t * t) * (GELU_A + 3.0 * GELU_B * square)
    for part, out in enumerate((d_query, d_key)):
        out[...] = jnp.concatenate([got[264 * h + 192:264 * h + 240, part * HS:(part + 1) * HS] for h in range(HEADS)], axis=1)
    rows = [got[264 * h + 240:264 * h + 264, :] for h in range(HEADS)]
    d_value[...] = jnp.concatenate([jnp.concatenate([r[:, :HS], r[:, HS:]], axis=0) for r in rows], axis=1)
    total = jnp.zeros((C, 2 * OWN), F32)
    for part in range(3):
        g = jnp.concatenate([got[264 * h + part * HS:264 * h + (part + 1) * HS, :] for h in range(HEADS)], axis=0)
        copies[part].wait()
        total += dot3_narrow(weights[part], g)
    d_xn = jnp.transpose(total)
    x = x_own[...]
    scale = rms_scale(x)
    xn = x * scale
    d_x = (dy[...] + scale * (d_xn - xn * jnp.mean(d_xn * xn, axis=-1, keepdims=True))) * (1.0 / POOL)
    hot_t = jnp.transpose(hot[:, :128].astype(F32)).astype(BF16)
    hot_two = jnp.concatenate([hot_t, hot_t], axis=1)
    summed = jnp.zeros((4 * KW, C), F32)
    for r in range(POOL):
        dh, dl = split2(d_x * slopes[:, r * C:(r + 1) * C])
        moved = dot(hot_two, jnp.concatenate([dh, dl], axis=0))
        summed += moved[4 * (r + 1):4 * (r + 1) + 4 * KW, :]
    dconv[...] = jnp.zeros_like(dconv)
    dconv[0:4 * KW, :] = summed
    sent[...] = jnp.transpose(dconv[:, pl.ds(pl.multiple_of(half * 384, 128), 384)])


def finish_kernel(parts, grads, d_conv, d_out, d_head):
    total = parts[0:48, :]
    for p in range(1, GROUP):
        total = total + parts[48 * p:48 * p + 48, :]
    padded = jnp.concatenate([total, jnp.zeros((80, 128), F32)], axis=0)
    d_conv[...] = jnp.transpose(padded)[:4 * KW, :48]
    d_out[...] = jnp.concatenate([grads[32 * j:32 * j + 32, :] for j in range(6)], axis=1)
    d_head[...] = grads[192:240, :]


def shape(*dims, dtype=F32):
    return jax.ShapeDtypeStruct(dims, dtype)


def params(mib=40):
    return pltpu.CompilerParams(vmem_limit_bytes=mib * 1024 * 1024)


def per_device(bases, targets, w_conv, w_query, w_key, w_value, w_out, w_head):
    s = lax.axis_index("seq")
    info = jnp.stack([lax.div(s, GROUP), lax.rem(s, GROUP)]).astype(jnp.int32)
    groups = [list(range(GROUP)), list(range(GROUP, 2 * GROUP))]

    def exchange(value):
        return lax.all_to_all(value, "seq", 0, 0, axis_index_groups=groups, tiled=True)

    targets_there = lax.ppermute(targets, "seq", [(i, i ^ GROUP) for i in range(2 * GROUP)])
    every = lax.all_to_all(jnp.broadcast_to(bases.reshape(1, 2, 128), (16, 2, 128)), "seq", 0, 0, tiled=True)

    xh, xl, x_own, hot_own, qkv, o_here = pl.pallas_call(
        attend_kernel,
        out_shape=(
            shape(TOKENS, C, dtype=BF16), shape(TOKENS, C, dtype=BF16), shape(2 * OWN, C), shape(2 * OWN, 256, dtype=BF16),
            shape(TOKENS, 3 * HS), shape(512, 128),
        ),
        in_specs=[SMEM, VMEM, VMEM, ANY, ANY, ANY],
        out_specs=(VMEM,) * 6,
        scratch_shapes=[
            pltpu.VMEM((POOL, WIN, C), F32),
            pltpu.VMEM((256, POOL * C), BF16),
            pltpu.VMEM((TOKENS + 16, 256), F32),
            pltpu.VMEM((3, C, 128), F32),
            pltpu.VMEM((TOKENS, C), F32),
            pltpu.VMEM((TOKENS, 256), BF16),
            pltpu.SemaphoreType.DMA((3,)),
        ],
        compiler_params=params(),
        name="attend",
    )(info, every, w_conv, w_query, w_key, w_value)

    log_rate, do_sent, dy, grads_part = pl.pallas_call(
        decode_kernel,
        out_shape=(shape(OWN, TRACKS), shape(HD, 128), shape(2 * OWN, C), shape(GROUP * 240, 128)),
        in_specs=[SMEM] + [VMEM] * 6,
        out_specs=(VMEM,) * 4,
        scratch_shapes=[pltpu.VMEM((2 * OWN, C), F32)],
        compiler_params=params(),
        name="decode",
    )(info, exchange(o_here), x_own, targets, targets_there, w_out, w_head)
    grads = lax.psum_scatter(grads_part, "seq", scatter_dimension=0, axis_index_groups=groups, tiled=True)

    sent = pl.pallas_call(
        attend_back_kernel,
        out_shape=shape(GROUP * 264, 128),
        in_specs=[SMEM, VMEM, VMEM, ANY, ANY],
        out_specs=VMEM,
        scratch_shapes=[
            pltpu.VMEM((TOKENS, 384), BF16),
            pltpu.VMEM((TOKENS, 384), BF16),
            pltpu.VMEM((TOKENS, HS), F32),
            pltpu.VMEM((3 * HS, TOKENS), F32),
            pltpu.VMEM((TOKENS, HS), F32),
            pltpu.VMEM((TOKENS, HS), F32),
            pltpu.SemaphoreType.DMA((2,)),
        ],
        compiler_params=params(),
        name="attend_back",
    )(info, exchange(do_sent), qkv, xh, xl)

    d_query, d_key, d_value, conv_sent = pl.pallas_call(
        encode_back_kernel,
        out_shape=(shape(48, HD), shape(48, HD), shape(48, HD), shape(GROUP * 48, 128)),
        in_specs=[SMEM, VMEM, ANY, ANY, ANY] + [VMEM] * 4,
        out_specs=(VMEM,) * 4,
        scratch_shapes=[
            pltpu.VMEM((POOL, WIN, C), F32),
            pltpu.VMEM((256, POOL * C), BF16),
            pltpu.VMEM((3, C, HD), F32),
            pltpu.VMEM((2 * OWN, POOL * C), F32),
            pltpu.VMEM((128, C), F32),
            pltpu.SemaphoreType.DMA((3,)),
        ],
        compiler_params=params(),
        name="encode_back",
    )(info, exchange(sent), w_query, w_key, w_value, w_conv, x_own, hot_own, dy)

    d_conv, d_out, d_head = pl.pallas_call(
        finish_kernel,
        out_shape=(shape(4 * KW, 48), shape(32, C), shape(48, TRACKS)),
        in_specs=[VMEM] * 2,
        out_specs=(VMEM,) * 3,
        compiler_params=params(16),
        name="finish",
    )(exchange(conv_sent), grads)
    return (log_rate, d_conv, d_query, d_key, d_value, d_out, d_head)


def solution(mesh):
    rows = P(("dp", "seq"), None)
    return jax.shard_map(
        per_device,
        mesh=mesh,
        in_specs=(P(("dp", "seq")), rows, P(), P(), P(), P(), P(), P()),
        out_specs=(rows, P("dp", "seq"), rows, rows, rows, rows, rows),
        check_vma=False,
    )
```

```python
import math

import jax
import jax.numpy as jnp
from jax import lax
from jax.experimental import pallas as pl
from jax.experimental.pallas import tpu as pltpu
from jax.sharding import PartitionSpec as P


C = 768
KW = 15
HEADS = 8
HS = 64
TRACKS = 128
POOL = 4
HD = 512
TOKENS = 1024
GROUP = 8
OWN = 64
F32 = jnp.float32
BF16 = jnp.bfloat16
GELU_A = math.sqrt(2.0 / math.pi)
GELU_B = GELU_A * 0.044715
WIN = 80
TILE = 256

VMEM = pl.BlockSpec(memory_space=pltpu.VMEM)
SMEM = pl.BlockSpec(memory_space=pltpu.SMEM)
ANY = pl.BlockSpec(memory_space=pl.ANY)


def dot(left, right):
    return lax.dot_general(left, right, (((1,), (0,)), ((), ())), preferred_element_type=F32)


def split2(a):
    hi = a.astype(BF16)
    return hi, (a - hi.astype(F32)).astype(BF16)


def split3(a):
    hi = a.astype(BF16)
    rest = a - hi.astype(F32)
    mid = rest.astype(BF16)
    return hi, mid, (rest - mid.astype(F32)).astype(BF16)


def dot3(left, right):
    lh, ll = split2(left)
    rh, rl = split2(right)
    return dot(lh, rh) + (dot(lh, rl) + dot(ll, rh))


def dot3_narrow(left, right):
    lh, ll = split2(left)
    rh, rl = split2(right)
    n = right.shape[1]
    both = dot(lh, jnp.concatenate([rh, rl], axis=1))
    return both[:, :n] + (both[:, n:] + dot(ll, rh))


def dot3_short(left, right):
    lh, ll = split2(left)
    rh, rl = split2(right)
    n = left.shape[0]
    both = dot(jnp.concatenate([lh, ll], axis=0), rh)
    return both[:n] + (both[n:] + dot(lh, rl))


def dot3_thin(left, right):
    lh, ll = split2(left)
    rh, rl = split2(right)
    return dot(jnp.concatenate([lh, lh, ll], axis=1), jnp.concatenate([rh, rl, rh], axis=0))


def dot6(left, right):
    lh, lm, ll = split3(left)
    rh, rm, rl = split3(right)
    return dot(lh, rh) + ((dot(lh, rm) + dot(lm, rh)) + (dot(lm, rm) + (dot(lh, rl) + dot(ll, rh))))


def rms_scale(a):
    return lax.rsqrt(jnp.mean(a * a, axis=-1, keepdims=True) + 1e-06)


def conv_weights(w_ref, pad_ref, out_ref):
    pad_ref[...] = jnp.zeros_like(pad_ref)
    for r in range(POOL):
        pad_ref[r, 4 * (r + 1):4 * (r + 1) + 4 * KW, :] = w_ref[...]
    for r in range(POOL):
        pieces = split3(pad_ref[r])
        zeros = jnp.zeros((256 - 3 * WIN, C), BF16)
        out_ref[:, r * C:(r + 1) * C] = jnp.concatenate([*pieces, zeros], axis=0)


def key_stack(k):
    h, m, l = split3(k)
    return jnp.concatenate([h, m, l, h, m, h], axis=1)


def query_stack(q_t):
    h, m, l = split3(q_t)
    return jnp.concatenate([h, h, h, m, m, l], axis=0)


def attend_kernel(
    info, bases, w_conv, wq_hbm, wk_hbm, wv_hbm,
    xh_out, xl_out, scale_out, x_own, hot_t, qkv_out, w_t, inverse, o_out, slopes_hbm, eh_hbm, el_hbm,
    pad, w_all, window, slabs, x_all, slopes, eh_all, el_all, sems, slope_sems, e_sems,
):
    half, m = info[0], info[1]
    copies = []
    for i, w in enumerate((wq_hbm, wk_hbm, wv_hbm)):
        lanes = pl.ds(pl.multiple_of(lax.div(m, 2) * 128, 128), 128)
        copies.append(pltpu.make_async_copy(w.at[:, lanes], slabs.at[i], sems.at[i]))
    for copy in copies:
        copy.start()
    conv_weights(w_conv, pad, w_all)

    lane = lax.broadcasted_iota(jnp.int32, (128, 256), 1)
    row = lax.broadcasted_iota(jnp.int32, (128, 256), 0)
    within = lax.rem(lane, WIN)
    place = lax.div(lax.rem(within, 16), 4)
    pick = jnp.where(lax.rem(row, 4) == place, 1.0, 0.0).astype(BF16)
    mine = lax.broadcasted_iota(jnp.int32, (32, 128), 0) == lax.div(lax.broadcasted_iota(jnp.int32, (32, 128), 1), 4)
    code = lax.rem(lax.broadcasted_iota(jnp.int32, (1, 256), 1), 4).astype(F32)
    window[0:8, :] = jnp.zeros((8, 256), F32)
    window[TOKENS + 8:TOKENS + 16, :] = jnp.zeros((8, 256), F32)
    for part in range(8):
        pieces = []
        for q in range(4 * part, 4 * part + 4):
            line = bases[q // 2, q % 2:q % 2 + 1, :].astype(F32)
            pieces.append(jnp.where(mine, jnp.broadcast_to(line, (32, 128)), 0.0))
        value = dot(jnp.concatenate(pieces, axis=0).astype(BF16), pick)
        window[8 + 128 * part:8 + 128 * part + 128, :] = jnp.where(value == code, 1.0, 0.0)

    shift = lax.div(lax.rem(lax.broadcasted_iota(jnp.int32, (TILE, 256), 1), WIN), 16)
    real = lax.broadcasted_iota(jnp.int32, (TILE, 256), 1) < 3 * WIN
    steps = TOKENS // TILE

    def encode(c, _):
        start = pl.multiple_of(lax.rem(c + half * (steps // 2), steps) * TILE, TILE)
        around = window[pl.ds(start, TILE + 16), :]
        hot = jnp.zeros((TILE, 256), F32)
        for d in range(5):
            hot = jnp.where(shift == d, around[6 + d:6 + d + TILE, :], hot)
        hot = jnp.where(real, hot, 0.0).astype(BF16)
        here = pl.ds(pl.multiple_of(c * TILE, TILE), TILE)
        total = jnp.zeros((TILE, C), F32)
        for r in range(POOL):
            pre = dot(hot, w_all[:, r * C:(r + 1) * C])
            square = pre * pre
            t = jnp.tanh(pre * (GELU_A + GELU_B * square))
            near = 0.5 + 0.5 * t
            total += pre * near
            slopes[here, r * C:(r + 1) * C] = near + pre * (near * (1.0 - t)) * (GELU_A + 3.0 * GELU_B * square)
        x_all[here, :] = total * (1.0 / POOL)
        hot_t[:, here] = jnp.transpose(hot[:, :128].astype(F32)).astype(BF16)
        pltpu.make_async_copy(slopes.at[here], slopes_hbm.at[here], slope_sems.at[c]).start()
        return 0

    lax.fori_loop(0, steps, encode, 0)
    for copy in copies:
        copy.wait()
    odd = lax.rem(m, 2) == 1
    columns = [jnp.where(odd, slabs[i, :, HS:], slabs[i, :, :HS]) for i in range(3)]
    w_t[...] = jnp.transpose(jnp.concatenate(columns, axis=1))
    w_qkv = jnp.concatenate([columns[0] * HS ** -0.5, columns[1], columns[2]], axis=1)
    wh, wm, wl = split3(w_qkv)

    def project(c, _):
        here = pl.ds(pl.multiple_of(c * TILE, TILE), TILE)
        x = x_all[here, :]
        scale = rms_scale(x)
        scale_out[here, :] = jnp.broadcast_to(scale, (TILE, 128))
        xn = x * scale
        h, mid, low = split3(xn)
        xh_out[here, :] = h
        xl_out[here, :] = mid
        qkv_out[here, :] = dot(h, wh) + ((dot(h, wm) + dot(mid, wh)) + (dot(mid, wm) + (dot(h, wl) + dot(low, wh))))
        return 0

    lax.fori_loop(0, steps, project, 0)
    for part in range(2):
        here = pl.ds(pl.multiple_of(part * 512 + m * OWN, OWN), OWN)
        x_own[part * OWN:(part + 1) * OWN, :] = x_all[here, :]

    qkv = qkv_out[...]
    q_t = query_stack(jnp.transpose(qkv[:, :HS]))
    keys = key_stack(qkv[:, HS:2 * HS])
    vh, vl = split2(jnp.transpose(qkv[:, 2 * HS:]))
    v_both = jnp.concatenate([vh, vl], axis=0)
    outs = []
    for c in range(steps):
        scores = dot(keys, q_t[:, c * TILE:(c + 1) * TILE])
        e = jnp.exp(scores - jnp.max(scores, axis=0, keepdims=True))
        eh, el = split2(e)
        over = 1.0 / jnp.sum(eh.astype(F32) + el.astype(F32), axis=0, keepdims=True)
        inverse[:, c * TILE:(c + 1) * TILE] = over
        eh_all[c] = eh
        el_all[c] = el
        for i, (here, there) in enumerate(((eh_all, eh_hbm), (el_all, el_hbm))):
            pltpu.make_async_copy(here.at[c], there.at[c], e_sems.at[i, c]).start()
        both = dot(v_both, eh)
        outs.append(jnp.transpose((both[:HS] + (both[HS:] + dot(vh, el))) * over))
    o_out[...] = jnp.concatenate(
        [jnp.concatenate(outs[:steps // 2], axis=0), jnp.concatenate(outs[steps // 2:], axis=0)], axis=1
    )
    for c in range(steps):
        here = pl.ds(c * TILE, TILE)
        pltpu.make_async_copy(slopes.at[here], slopes_hbm.at[here], slope_sems.at[c]).wait()
        pltpu.make_async_copy(eh_all.at[c], eh_hbm.at[c], e_sems.at[0, c]).wait()
        pltpu.make_async_copy(el_all.at[c], el_hbm.at[c], e_sems.at[1, c]).wait()


def decode_kernel(
    info, o_parts, x_own, targets_here, targets_there, w_out, w_head,
    log_rate, do_out, dy_out, shared_hbm, yn_all, grads_out, sem,
):
    half = info[0]
    parts = [o_parts[h * OWN:(h + 1) * OWN, :] for h in range(HEADS)]
    attended = jnp.concatenate(
        [jnp.concatenate([p[:, :HS] for p in parts], axis=1), jnp.concatenate([p[:, HS:] for p in parts], axis=1)], axis=0
    )
    wout = w_out[...]
    wouth, woutl = split2(wout)
    ah, al = split2(attended)
    both = dot(jnp.concatenate([ah, al], axis=0), wouth)
    y = x_own[...] + (both[:2 * OWN] + (both[2 * OWN:] + dot(ah, woutl)))
    scale = rms_scale(y)
    yn = y * scale
    yn_all[...] = yn
    rate = dot3_narrow(yn, w_head[...])
    log_rate[...] = rate[:OWN]
    targets = jnp.concatenate([targets_here[...], targets_there[...]], axis=0).astype(F32)
    d_rate = (jnp.exp(rate) - targets) * (1.0 / math.sqrt(TOKENS))
    d_yn = dot3_thin(d_rate, jnp.transpose(w_head[...]))
    dy = scale * (d_yn - yn * jnp.mean(d_yn * yn, axis=-1, keepdims=True))
    dy_out[...] = dy
    dth, dtl = split2(jnp.transpose(dy))
    both = dot(wouth, jnp.concatenate([dth, dtl], axis=1))
    do_out[...] = both[:, :2 * OWN] + (both[:, 2 * OWN:] + dot(woutl, dth))

    heads = o_parts[pl.ds(pl.multiple_of(half * 256, 256), 256), :]
    o_t = jnp.concatenate(
        [
            jnp.concatenate(
                [jnp.transpose(heads[h * OWN:(h + 1) * OWN, :])[:HS], jnp.transpose(heads[h * OWN:(h + 1) * OWN, :])[HS:]], axis=1
            )
            for h in range(4)
        ],
        axis=0,
    )
    d_out = dot3_thin(o_t, dy)
    yn_half = yn_all[:, pl.ds(pl.multiple_of(half * 384, 128), 384)]
    d_head = dot3_thin(jnp.transpose(yn_half), d_rate)
    for p in range(GROUP):
        for j in range(6):
            grads_out[p, 32 * j:32 * j + 32, :] = d_out[32 * p:32 * p + 32, 128 * j:128 * j + 128]
        grads_out[p, 192:240, :] = d_head[48 * p:48 * p + 48, :]
    copy = pltpu.make_async_copy(grads_out, shared_hbm.at[:, 96:336], sem)
    copy.start()
    copy.wait()


def attend_back_kernel(
    info, do_parts, qkv_ref, inverse, w_t, hot_t, scales, dy, eh_hbm, el_hbm, xh_hbm, xl_hbm, slopes_hbm, _,
    shared_hbm,
    sent, eh_all, el_all, xh, xl, slopes, do_all, g_t, dk_acc, dv_acc, dy_all, conv_acc, dconv, sems, e_sems, sent_sem,
):
    half, m = info[0], info[1]
    steps = TOKENS // TILE
    e_copies = [
        [pltpu.make_async_copy(there.at[c], here.at[c], e_sems.at[i, c]) for i, (there, here) in enumerate(((eh_hbm, eh_all), (el_hbm, el_all)))]
        for c in range(steps)
    ]
    copies = [pltpu.make_async_copy(a, b, sems.at[i]) for i, (a, b) in enumerate(((xh_hbm, xh), (xl_hbm, xl), (slopes_hbm, slopes)))]
    for pair in e_copies:
        for copy in pair:
            copy.start()
    for copy in copies:
        copy.start()
    for p in range(GROUP):
        both = jnp.transpose(do_parts[p * OWN:(p + 1) * OWN, :])
        do_all[p * OWN:(p + 1) * OWN, :] = both[:OWN]
        do_all[512 + p * OWN:512 + (p + 1) * OWN, :] = both[OWN:]
    qkv = qkv_ref[...]
    kh, kl = split2(jnp.transpose(qkv[:, HS:2 * HS]))
    k_both = jnp.concatenate([kh, kl], axis=0)
    vh, vl = split2(qkv[:, 2 * HS:])
    v_three = jnp.concatenate([vh, vh, vl], axis=1)
    turned = jnp.transpose(do_all[...])
    dth, dtl = split2(turned)
    do_t = jnp.concatenate([dth, dtl, dth], axis=0)
    dh, dl = split2(jnp.transpose(turned * inverse[...]))
    do_both = jnp.concatenate([dh, dl], axis=1)
    qh, ql = split2(qkv[:, :HS])
    q_both = jnp.concatenate([qh, ql], axis=1)
    dy_all[...] = jnp.zeros_like(dy_all)
    for part in range(2):
        dy_all[pl.ds(pl.multiple_of(part * 512 + m * OWN, OWN), OWN), :] = dy[part * OWN:(part + 1) * OWN, :]
    for c in range(steps):
        here = slice(c * TILE, (c + 1) * TILE)
        dp = dot(v_three, do_t[:, here])
        for copy in e_copies[c]:
            copy.wait()
        eh, el = eh_all[c], el_all[c]
        p = (eh.astype(F32) + el.astype(F32)) * inverse[:, here]
        ds = p * (dp - jnp.sum(p * dp, axis=0, keepdims=True))
        sh, sl = split2(ds)
        both = dot(k_both, sh)
        g_t[0:HS, here] = (both[:HS] + (both[HS:] + dot(kh, sl))) * (HS ** -0.5)
        both = dot(eh, do_both[here])
        dv = both[:, :HS] + (both[:, HS:] + dot(el, dh[here]))
        both = dot(sh, q_both[here])
        dk = both[:, :HS] + (both[:, HS:] + dot(sl, qh[here]))
        if c == 0:
            dk_acc[...] = dk
            dv_acc[...] = dv
        else:
            dk_acc[...] += dk
            dv_acc[...] += dv
    g_t[HS:2 * HS, :] = jnp.transpose(dk_acc[...])
    g_t[2 * HS:3 * HS, :] = jnp.transpose(dv_acc[...])
    for copy in copies:
        copy.wait()
    lanes = pl.ds(pl.multiple_of(half * 384, 128), 384)
    gh, gl = split2(g_t[...])
    both = dot(jnp.concatenate([gh, gl], axis=0), xh[:, lanes])
    d_w = jnp.transpose(both[:192] + (both[192:] + dot(gh, xl[:, lanes])))

    wh, wl = split2(w_t[...])
    w_three = jnp.concatenate([wh, wl, wh], axis=0)
    for c in range(steps):
        here = slice(c * TILE, (c + 1) * TILE)
        gh, gl = split2(jnp.transpose(g_t[:, here]))
        d_xn = dot(jnp.concatenate([gh, gh, gl], axis=1), w_three)
        xn = xh[here].astype(F32) + xl[here].astype(F32)
        mean = jnp.mean(d_xn * xn, axis=-1, keepdims=True)
        d_x = (dy_all[here] + scales[here, :1] * (d_xn - xn * mean)) * (1.0 / POOL)
        hot = hot_t[:, here]
        hot_two = jnp.concatenate([hot, hot], axis=1)
        for r in range(POOL):
            dh, dl = split2(d_x * slopes[here, r * C:(r + 1) * C])
            moved = dot(hot_two, jnp.concatenate([dh, dl], axis=0))
            if c == 0:
                conv_acc[r] = moved
            else:
                conv_acc[r] += moved
    summed = conv_acc[0, 4:4 + 4 * KW, :]
    for r in range(1, POOL):
        summed += conv_acc[r, 4 * (r + 1):4 * (r + 1) + 4 * KW, :]
    dconv[...] = jnp.zeros_like(dconv)
    dconv[0:4 * KW, :] = summed
    d_conv = jnp.transpose(dconv[:, lanes])
    for p in range(GROUP):
        mine = d_w[48 * p:48 * p + 48, :]
        sent[p, 0:48, :] = mine[:, :128]
        sent[p, 48:72, :] = jnp.concatenate([mine[:24, 128:], mine[24:, 128:]], axis=1)
        mine = d_conv[48 * p:48 * p + 48, :HS]
        sent[p, 72:96, :] = jnp.concatenate([mine[:24], mine[24:]], axis=1)
    copy = pltpu.make_async_copy(sent, shared_hbm.at[:, 0:96], sent_sem)
    copy.start()
    copy.wait()


def finish_kernel(got, d_conv, d_query, d_key, d_value, d_out, d_head):
    total = got[0, 72:96, :]
    every = got[0, 96:336, :]
    for p in range(1, GROUP):
        total = total + got[p, 72:96, :]
        every = every + got[p, 96:336, :]
    d_conv[...] = jnp.concatenate([total[:, :HS], total[:, HS:]], axis=0)[:, :4 * KW]
    d_out[...] = jnp.concatenate([every[32 * j:32 * j + 32, :] for j in range(6)], axis=1)
    d_head[...] = every[192:240, :]
    for part, out in enumerate((d_query, d_key)):
        out[...] = jnp.concatenate([got[h, 0:48, part * HS:(part + 1) * HS] for h in range(HEADS)], axis=1)
    rows = [got[h, 48:72, :] for h in range(HEADS)]
    d_value[...] = jnp.concatenate([jnp.concatenate([r[:, :HS], r[:, HS:]], axis=0) for r in rows], axis=1)


def shape(*dims, dtype=F32):
    return jax.ShapeDtypeStruct(dims, dtype)


def params(mib=60):
    return pltpu.CompilerParams(vmem_limit_bytes=mib * 1024 * 1024)


def per_device(bases, targets, w_conv, w_query, w_key, w_value, w_out, w_head):
    s = lax.axis_index("seq")
    info = jnp.stack([lax.div(s, GROUP), lax.rem(s, GROUP)]).astype(jnp.int32)
    groups = [list(range(GROUP)), list(range(GROUP, 2 * GROUP))]

    def exchange(value):
        return lax.all_to_all(value, "seq", 0, 0, axis_index_groups=groups, tiled=True)

    targets_there = lax.ppermute(targets, "seq", [(i, i ^ GROUP) for i in range(2 * GROUP)])
    every = lax.all_to_all(jnp.broadcast_to(bases.reshape(1, 2, 128), (16, 2, 128)), "seq", 0, 0, tiled=True)

    xh, xl, scales, x_own, hot_t, qkv, w_t, inverse, o_here, slopes, eh, el = pl.pallas_call(
        attend_kernel,
        out_shape=(
            shape(TOKENS, C, dtype=BF16), shape(TOKENS, C, dtype=BF16), shape(TOKENS, 128), shape(2 * OWN, C),
            shape(128, TOKENS, dtype=BF16), shape(TOKENS, 3 * HS), shape(3 * HS, C), shape(1, TOKENS), shape(512, 128),
            shape(TOKENS, POOL * C), shape(4, TOKENS, TILE, dtype=BF16), shape(4, TOKENS, TILE, dtype=BF16),
        ),
        in_specs=[SMEM, VMEM, VMEM, ANY, ANY, ANY],
        out_specs=(VMEM,) * 9 + (ANY,) * 3,
        scratch_shapes=[
            pltpu.VMEM((POOL, WIN, C), F32),
            pltpu.VMEM((256, POOL * C), BF16),
            pltpu.VMEM((TOKENS + 16, 256), F32),
            pltpu.VMEM((3, C, 128), F32),
            pltpu.VMEM((TOKENS, C), F32),
            pltpu.VMEM((TOKENS, POOL * C), F32),
            pltpu.VMEM((4, TOKENS, TILE), BF16),
            pltpu.VMEM((4, TOKENS, TILE), BF16),
            pltpu.SemaphoreType.DMA((3,)),
            pltpu.SemaphoreType.DMA((4,)),
            pltpu.SemaphoreType.DMA((2, 4)),
        ],
        compiler_params=params(),
        name="attend",
    )(info, every, w_conv, w_query, w_key, w_value)

    log_rate, do_sent, dy, shared = pl.pallas_call(
        decode_kernel,
        out_shape=(shape(OWN, TRACKS), shape(HD, 128), shape(2 * OWN, C), shape(GROUP, 336, 128)),
        in_specs=[SMEM] + [VMEM] * 6,
        out_specs=(VMEM,) * 3 + (ANY,),
        scratch_shapes=[pltpu.VMEM((2 * OWN, C), F32), pltpu.VMEM((GROUP, 240, 128), F32), pltpu.SemaphoreType.DMA],
        compiler_params=params(),
        name="decode",
    )(info, exchange(o_here), x_own, targets, targets_there, w_out, w_head)

    sent = pl.pallas_call(
        attend_back_kernel,
        out_shape=shape(GROUP, 336, 128),
        in_specs=[SMEM] + [VMEM] * 7 + [ANY] * 6,
        out_specs=ANY,
        input_output_aliases={13: 0},
        scratch_shapes=[
            pltpu.VMEM((GROUP, 96, 128), F32),
            pltpu.VMEM((4, TOKENS, TILE), BF16),
            pltpu.VMEM((4, TOKENS, TILE), BF16),
            pltpu.VMEM((TOKENS, C), BF16),
            pltpu.VMEM((TOKENS, C), BF16),
            pltpu.VMEM((TOKENS, POOL * C), F32),
            pltpu.VMEM((TOKENS, HS), F32),
            pltpu.VMEM((3 * HS, TOKENS), F32),
            pltpu.VMEM((TOKENS, HS), F32),
            pltpu.VMEM((TOKENS, HS), F32),
            pltpu.VMEM((TOKENS, C), F32),
            pltpu.VMEM((POOL, 128, C), F32),
            pltpu.VMEM((128, C), F32),
            pltpu.SemaphoreType.DMA((3,)),
            pltpu.SemaphoreType.DMA((2, 4)),
            pltpu.SemaphoreType.DMA,
        ],
        compiler_params=params(),
        name="attend_back",
    )(info, exchange(do_sent), qkv, inverse, w_t, hot_t, scales, dy, eh, el, xh, xl, slopes, shared)

    d_conv, d_query, d_key, d_value, d_out, d_head = pl.pallas_call(
        finish_kernel,
        out_shape=(shape(48, 4 * KW), shape(48, HD), shape(48, HD), shape(48, HD), shape(32, C), shape(48, TRACKS)),
        in_specs=[VMEM],
        out_specs=(VMEM,) * 6,
        compiler_params=params(),
        name="finish",
    )(exchange(sent))
    return (log_rate, jnp.transpose(d_conv), d_query, d_key, d_value, d_out, d_head)


def solution(mesh):
    rows = P(("dp", "seq"), None)
    return jax.shard_map(
        per_device,
        mesh=mesh,
        in_specs=(P(("dp", "seq")), rows, P(), P(), P(), P(), P(), P()),
        out_specs=(rows, P("dp", "seq"), rows, rows, rows, rows, rows),
        check_vma=False,
    )
```

```python
import math

import jax
import jax.numpy as jnp
from jax import lax
from jax.experimental import pallas as pl
from jax.experimental.pallas import tpu as pltpu
from jax.sharding import PartitionSpec as P


C = 768
KW = 15
HEADS = 8
HS = 64
TRACKS = 128
POOL = 4
HD = 512
TOKENS = 1024
GROUP = 8
OWN = 64
F32 = jnp.float32
BF16 = jnp.bfloat16
GELU_A = math.sqrt(2.0 / math.pi)
GELU_C = 0.044715 / GELU_A ** 2
WIN = 80
TILE = 256

VMEM = pl.BlockSpec(memory_space=pltpu.VMEM)
SMEM = pl.BlockSpec(memory_space=pltpu.SMEM)
ANY = pl.BlockSpec(memory_space=pl.ANY)


def dot(left, right):
    return lax.dot_general(left, right, (((1,), (0,)), ((), ())), preferred_element_type=F32)


def split2(a):
    hi = a.astype(BF16)
    return hi, (a - hi.astype(F32)).astype(BF16)


def split3(a):
    hi = a.astype(BF16)
    rest = a - hi.astype(F32)
    mid = rest.astype(BF16)
    return hi, mid, (rest - mid.astype(F32)).astype(BF16)


def dot3(left, right):
    lh, ll = split2(left)
    rh, rl = split2(right)
    return dot(lh, rh) + (dot(lh, rl) + dot(ll, rh))


def dot3_narrow(left, right):
    lh, ll = split2(left)
    rh, rl = split2(right)
    n = right.shape[1]
    both = dot(lh, jnp.concatenate([rh, rl], axis=1))
    return both[:, :n] + (both[:, n:] + dot(ll, rh))


def dot3_short(left, right):
    lh, ll = split2(left)
    rh, rl = split2(right)
    n = left.shape[0]
    both = dot(jnp.concatenate([lh, ll], axis=0), rh)
    return both[:n] + (both[n:] + dot(lh, rl))


def dot3_thin(left, right):
    lh, ll = split2(left)
    rh, rl = split2(right)
    return dot(jnp.concatenate([lh, lh, ll], axis=1), jnp.concatenate([rh, rl, rh], axis=0))


def dot6(left, right):
    lh, lm, ll = split3(left)
    rh, rm, rl = split3(right)
    return dot(lh, rh) + ((dot(lh, rm) + dot(lm, rh)) + (dot(lm, rm) + (dot(lh, rl) + dot(ll, rh))))


def rms_scale(a):
    return lax.rsqrt(jnp.mean(a * a, axis=-1, keepdims=True) + 1e-06)


def conv_weights(w_ref, pad_ref, out_ref):
    pad_ref[...] = jnp.zeros_like(pad_ref)
    for r in range(POOL):
        pad_ref[r, 4 * (r + 1):4 * (r + 1) + 4 * KW, :] = w_ref[...] * GELU_A
    for r in range(POOL):
        pieces = split3(pad_ref[r])
        zeros = jnp.zeros((256 - 3 * WIN, C), BF16)
        out_ref[:, r * C:(r + 1) * C] = jnp.concatenate([*pieces, zeros], axis=0)


def key_stack(k):
    h, m, l = split3(k)
    return jnp.concatenate([h, m, l, h, m, h], axis=1)


def query_stack(q_t):
    h, m, l = split3(q_t)
    return jnp.concatenate([h, h, h, m, m, l], axis=0)


def attend_kernel(
    info, bases, w_conv, wq_hbm, wk_hbm, wv_hbm,
    x_own, hot_t, inverse, o_out, xh_hbm, xl_hbm, scale_hbm, qkv_hbm, w_t_hbm, slopes_hbm, eh_hbm, el_hbm,
    pad, w_all, window, slabs, x_all, xh_out, xl_out, scale_out, qkv_out, w_t, slopes, eh_all, el_all, sems, slope_sems, e_sems, out_sems,
):
    half, m = info[0], info[1]
    copies = []
    for i, w in enumerate((wq_hbm, wk_hbm, wv_hbm)):
        lanes = pl.ds(pl.multiple_of(lax.div(m, 2) * 128, 128), 128)
        copies.append(pltpu.make_async_copy(w.at[:, lanes], slabs.at[i], sems.at[i]))
    for copy in copies:
        copy.start()
    conv_weights(w_conv, pad, w_all)

    lane = lax.broadcasted_iota(jnp.int32, (128, 256), 1)
    row = lax.broadcasted_iota(jnp.int32, (128, 256), 0)
    within = lax.rem(lane, WIN)
    place = lax.div(lax.rem(within, 16), 4)
    pick = jnp.where(lax.rem(row, 4) == place, 1.0, 0.0).astype(BF16)
    mine = lax.broadcasted_iota(jnp.int32, (32, 128), 0) == lax.div(lax.broadcasted_iota(jnp.int32, (32, 128), 1), 4)
    code = lax.rem(lax.broadcasted_iota(jnp.int32, (1, 256), 1), 4).astype(F32)
    window[0:8, :] = jnp.zeros((8, 256), F32)
    window[TOKENS + 8:TOKENS + 16, :] = jnp.zeros((8, 256), F32)
    for part in range(8):
        pieces = []
        for q in range(4 * part, 4 * part + 4):
            line = bases[q // 2, q % 2:q % 2 + 1, :].astype(F32)
            pieces.append(jnp.where(mine, jnp.broadcast_to(line, (32, 128)), 0.0))
        value = dot(jnp.concatenate(pieces, axis=0).astype(BF16), pick)
        window[8 + 128 * part:8 + 128 * part + 128, :] = jnp.where(value == code, 1.0, 0.0)

    shift = lax.div(lax.rem(lax.broadcasted_iota(jnp.int32, (TILE, 256), 1), WIN), 16)
    real = lax.broadcasted_iota(jnp.int32, (TILE, 256), 1) < 3 * WIN
    steps = TOKENS // TILE

    def encode(c, _):
        start = pl.multiple_of(lax.rem(c + half * (steps // 2), steps) * TILE, TILE)
        around = window[pl.ds(start, TILE + 16), :]
        hot = jnp.zeros((TILE, 256), F32)
        for d in range(5):
            hot = jnp.where(shift == d, around[6 + d:6 + d + TILE, :], hot)
        hot = jnp.where(real, hot, 0.0).astype(BF16)
        here = pl.ds(pl.multiple_of(c * TILE, TILE), TILE)
        total = None
        for r in range(POOL):
            y = dot(hot, w_all[:, r * C:(r + 1) * C])
            b = y * y * GELU_C
            t = jnp.tanh(y + y * b)
            up = 1.0 + t
            total = y * up if total is None else total + y * up
            slopes[here, r * C:(r + 1) * C] = up + (1.0 - t * t) * (y + y * (3.0 * b))
        x_all[here, :] = total * (0.5 / (GELU_A * POOL))
        hot_t[:, here] = jnp.transpose(hot[:, :128].astype(F32)).astype(BF16)
        pltpu.make_async_copy(slopes.at[here], slopes_hbm.at[here], slope_sems.at[c]).start()
        return 0

    lax.fori_loop(0, steps, encode, 0)
    for copy in copies:
        copy.wait()
    odd = lax.rem(m, 2) == 1
    columns = [jnp.where(odd, slabs[i, :, HS:], slabs[i, :, :HS]) for i in range(3)]
    w_t[...] = jnp.transpose(jnp.concatenate(columns, axis=1))
    w_qkv = jnp.concatenate([columns[0] * HS ** -0.5, columns[1], columns[2]], axis=1)
    wh, wm, wl = split3(w_qkv)

    def project(c, _):
        here = pl.ds(pl.multiple_of(c * TILE, TILE), TILE)
        x = x_all[here, :]
        scale = rms_scale(x)
        scale_out[here, :] = jnp.broadcast_to(scale, (TILE, 128))
        xn = x * scale
        h, mid, low = split3(xn)
        xh_out[here, :] = h
        xl_out[here, :] = mid
        qkv_out[here, :] = dot(h, wh) + ((dot(h, wm) + dot(mid, wh)) + (dot(mid, wm) + (dot(h, wl) + dot(low, wh))))
        return 0

    lax.fori_loop(0, steps, project, 0)
    for part in range(2):
        here = pl.ds(pl.multiple_of(part * 512 + m * OWN, OWN), OWN)
        x_own[part * OWN:(part + 1) * OWN, :] = x_all[here, :]

    outs_copies = [
        pltpu.make_async_copy(a, b, out_sems.at[i])
        for i, (a, b) in enumerate(((xh_out, xh_hbm), (xl_out, xl_hbm), (scale_out, scale_hbm), (qkv_out, qkv_hbm), (w_t, w_t_hbm)))
    ]
    for copy in outs_copies:
        copy.start()
    qkv = qkv_out[...]
    q_t = query_stack(jnp.transpose(qkv[:, :HS]))
    keys = key_stack(qkv[:, HS:2 * HS])
    vh, vl = split2(jnp.transpose(qkv[:, 2 * HS:]))
    v_both = jnp.concatenate([vh, vl], axis=0)
    outs = []
    for c in range(steps):
        scores = dot(keys, q_t[:, c * TILE:(c + 1) * TILE])
        e = jnp.exp(scores - jnp.max(scores, axis=0, keepdims=True))
        eh, el = split2(e)
        over = 1.0 / jnp.sum(eh.astype(F32) + el.astype(F32), axis=0, keepdims=True)
        inverse[:, c * TILE:(c + 1) * TILE] = over
        eh_all[c] = eh
        el_all[c] = el
        for i, (here, there) in enumerate(((eh_all, eh_hbm), (el_all, el_hbm))):
            pltpu.make_async_copy(here.at[c], there.at[c], e_sems.at[i, c]).start()
        both = dot(v_both, eh)
        outs.append(jnp.transpose((both[:HS] + (both[HS:] + dot(vh, el))) * over))
    o_out[...] = jnp.concatenate(
        [jnp.concatenate(outs[:steps // 2], axis=0), jnp.concatenate(outs[steps // 2:], axis=0)], axis=1
    )
    for copy in outs_copies:
        copy.wait()
    for c in range(steps):
        here = pl.ds(c * TILE, TILE)
        pltpu.make_async_copy(slopes.at[here], slopes_hbm.at[here], slope_sems.at[c]).wait()
        pltpu.make_async_copy(eh_all.at[c], eh_hbm.at[c], e_sems.at[0, c]).wait()
        pltpu.make_async_copy(el_all.at[c], el_hbm.at[c], e_sems.at[1, c]).wait()


def decode_kernel(
    info, o_parts, x_own, targets_here, targets_there, w_out, w_head,
    log_rate, do_out, dy_out, grads_hbm, yn_all, grads_out, sem,
):
    half = info[0]
    parts = [o_parts[h * OWN:(h + 1) * OWN, :] for h in range(HEADS)]
    attended = jnp.concatenate(
        [jnp.concatenate([p[:, :HS] for p in parts], axis=1), jnp.concatenate([p[:, HS:] for p in parts], axis=1)], axis=0
    )
    wout = w_out[...]
    wouth, woutl = split2(wout)
    ah, al = split2(attended)
    both = dot(jnp.concatenate([ah, al], axis=0), wouth)
    y = x_own[...] + (both[:2 * OWN] + (both[2 * OWN:] + dot(ah, woutl)))
    scale = rms_scale(y)
    yn = y * scale
    yn_all[...] = yn
    rate = dot3_narrow(yn, w_head[...])
    log_rate[...] = rate[:OWN]
    targets = jnp.concatenate([targets_here[...], targets_there[...]], axis=0).astype(F32)
    d_rate = (jnp.exp(rate) - targets) * (1.0 / math.sqrt(TOKENS))
    d_yn = dot3_thin(d_rate, jnp.transpose(w_head[...]))
    dy = scale * (d_yn - yn * jnp.mean(d_yn * yn, axis=-1, keepdims=True))
    dy_out[...] = dy
    heads = o_parts[pl.ds(pl.multiple_of(half * 256, 256), 256), :]
    o_t = jnp.concatenate(
        [
            jnp.concatenate(
                [jnp.transpose(heads[h * OWN:(h + 1) * OWN, :])[:HS], jnp.transpose(heads[h * OWN:(h + 1) * OWN, :])[HS:]], axis=1
            )
            for h in range(4)
        ],
        axis=0,
    )
    d_out = dot3_thin(o_t, dy)
    yn_half = yn_all[:, pl.ds(pl.multiple_of(half * 384, 128), 384)]
    d_head = dot3_thin(jnp.transpose(yn_half), d_rate)
    for p in range(GROUP):
        for j in range(6):
            grads_out[p, 32 * j:32 * j + 32, :] = d_out[32 * p:32 * p + 32, 128 * j:128 * j + 128]
        grads_out[p, 192:240, :] = d_head[48 * p:48 * p + 48, :]
    copy = pltpu.make_async_copy(grads_out, grads_hbm, sem)
    copy.start()
    dth, dtl = split2(jnp.transpose(dy))
    both = dot(wouth, jnp.concatenate([dth, dtl], axis=1))
    do_out[...] = both[:, :2 * OWN] + (both[:, 2 * OWN:] + dot(woutl, dth))
    copy.wait()


def attend_back_kernel(
    info, do_parts, qkv_ref, inverse, w_t, hot_t, scales, dy, eh_hbm, el_hbm, xh_hbm, xl_hbm, slopes_hbm,
    sent,
    eh_all, el_all, xh, xl, slopes, do_all, g_t, dk_acc, dv_acc, dy_all, conv_acc, dconv, sems, e_sems,
):
    half, m = info[0], info[1]
    steps = TOKENS // TILE
    e_copies = [
        [pltpu.make_async_copy(there.at[c], here.at[c], e_sems.at[i, c]) for i, (there, here) in enumerate(((eh_hbm, eh_all), (el_hbm, el_all)))]
        for c in range(steps)
    ]
    copies = [pltpu.make_async_copy(a, b, sems.at[i]) for i, (a, b) in enumerate(((xh_hbm, xh), (xl_hbm, xl)))]
    copies += [
        pltpu.make_async_copy(slopes_hbm.at[pl.ds(c * TILE, TILE)], slopes.at[pl.ds(c * TILE, TILE)], sems.at[2 + c]) for c in range(steps)
    ]
    for pair in e_copies:
        for copy in pair:
            copy.start()
    for copy in copies:
        copy.start()
    for p in range(GROUP):
        both = jnp.transpose(do_parts[p * OWN:(p + 1) * OWN, :])
        do_all[p * OWN:(p + 1) * OWN, :] = both[:OWN]
        do_all[512 + p * OWN:512 + (p + 1) * OWN, :] = both[OWN:]
    qkv = qkv_ref[...]
    kh, kl = split2(jnp.transpose(qkv[:, HS:2 * HS]))
    k_both = jnp.concatenate([kh, kl], axis=0)
    vh, vl = split2(qkv[:, 2 * HS:])
    v_three = jnp.concatenate([vh, vh, vl], axis=1)
    turned = jnp.transpose(do_all[...])
    dth, dtl = split2(turned)
    do_t = jnp.concatenate([dth, dtl, dth], axis=0)
    dh, dl = split2(jnp.transpose(turned * inverse[...]))
    do_both = jnp.concatenate([dh, dl], axis=1)
    qh, ql = split2(qkv[:, :HS])
    q_both = jnp.concatenate([qh, ql], axis=1)
    dy_all[...] = jnp.zeros_like(dy_all)
    for part in range(2):
        dy_all[pl.ds(pl.multiple_of(part * 512 + m * OWN, OWN), OWN), :] = dy[part * OWN:(part + 1) * OWN, :]
    for c in range(steps):
        here = slice(c * TILE, (c + 1) * TILE)
        dp = dot(v_three, do_t[:, here])
        for copy in e_copies[c]:
            copy.wait()
        eh, el = eh_all[c], el_all[c]
        p = (eh.astype(F32) + el.astype(F32)) * inverse[:, here]
        ds = p * (dp - jnp.sum(p * dp, axis=0, keepdims=True))
        sh, sl = split2(ds)
        both = dot(k_both, sh)
        g_t[0:HS, here] = (both[:HS] + (both[HS:] + dot(kh, sl))) * (HS ** -0.5)
        both = dot(eh, do_both[here])
        dv = both[:, :HS] + (both[:, HS:] + dot(el, dh[here]))
        both = dot(sh, q_both[here])
        dk = both[:, :HS] + (both[:, HS:] + dot(sl, qh[here]))
        if c == 0:
            dk_acc[...] = dk
            dv_acc[...] = dv
        else:
            dk_acc[...] += dk
            dv_acc[...] += dv
    g_t[HS:2 * HS, :] = jnp.transpose(dk_acc[...])
    g_t[2 * HS:3 * HS, :] = jnp.transpose(dv_acc[...])
    copies[0].wait()
    copies[1].wait()
    lanes = pl.ds(pl.multiple_of(half * 384, 128), 384)
    gh, gl = split2(g_t[...])
    both = dot(jnp.concatenate([gh, gl], axis=0), xh[:, lanes])
    d_w = jnp.transpose(both[:192] + (both[192:] + dot(gh, xl[:, lanes])))

    wh, wl = split2(w_t[...])
    w_three = jnp.concatenate([wh, wl, wh], axis=0)
    for c in range(steps):
        here = slice(c * TILE, (c + 1) * TILE)
        gh, gl = split2(jnp.transpose(g_t[:, here]))
        d_xn = dot(jnp.concatenate([gh, gh, gl], axis=1), w_three)
        xn = xh[here].astype(F32) + xl[here].astype(F32)
        mean = jnp.mean(d_xn * xn, axis=-1, keepdims=True)
        d_x = (dy_all[here] + scales[here, :1] * (d_xn - xn * mean)) * (0.5 / POOL)
        copies[2 + c].wait()
        hot = hot_t[:, here]
        hot_two = jnp.concatenate([hot, hot], axis=1)
        for r in range(POOL):
            dh, dl = split2(d_x * slopes[here, r * C:(r + 1) * C])
            moved = dot(hot_two, jnp.concatenate([dh, dl], axis=0))
            if c == 0:
                conv_acc[r] = moved
            else:
                conv_acc[r] += moved
    summed = conv_acc[0, 4:4 + 4 * KW, :]
    for r in range(1, POOL):
        summed += conv_acc[r, 4 * (r + 1):4 * (r + 1) + 4 * KW, :]
    dconv[...] = jnp.zeros_like(dconv)
    dconv[0:4 * KW, :] = summed
    d_conv = jnp.transpose(dconv[:, lanes])
    for p in range(GROUP):
        mine = d_w[48 * p:48 * p + 48, :]
        sent[p, 0:48, :] = mine[:, :128]
        sent[p, 48:72, :] = jnp.concatenate([mine[:24, 128:], mine[24:, 128:]], axis=1)
        mine = d_conv[48 * p:48 * p + 48, :HS]
        sent[p, 72:96, :] = jnp.concatenate([mine[:24], mine[24:]], axis=1)


def finish_kernel(got, grads, d_conv, d_query, d_key, d_value, d_out, d_head):
    total = got[0, 72:96, :]
    every = grads[0]
    for p in range(1, GROUP):
        total = total + got[p, 72:96, :]
        every = every + grads[p]
    d_conv[...] = jnp.concatenate([total[:, :HS], total[:, HS:]], axis=0)[:, :4 * KW]
    d_out[...] = jnp.concatenate([every[32 * j:32 * j + 32, :] for j in range(6)], axis=1)
    d_head[...] = every[192:240, :]
    for part, out in enumerate((d_query, d_key)):
        out[...] = jnp.concatenate([got[h, 0:48, part * HS:(part + 1) * HS] for h in range(HEADS)], axis=1)
    rows = [got[h, 48:72, :] for h in range(HEADS)]
    d_value[...] = jnp.concatenate([jnp.concatenate([r[:, :HS], r[:, HS:]], axis=0) for r in rows], axis=1)


def shape(*dims, dtype=F32):
    return jax.ShapeDtypeStruct(dims, dtype)


def params(mib=60):
    return pltpu.CompilerParams(vmem_limit_bytes=mib * 1024 * 1024)


def attend():
    return pl.pallas_call(
        attend_kernel,
        out_shape=(
            shape(2 * OWN, C), shape(128, TOKENS, dtype=BF16), shape(1, TOKENS), shape(512, 128),
            shape(TOKENS, C, dtype=BF16), shape(TOKENS, C, dtype=BF16), shape(TOKENS, 128), shape(TOKENS, 3 * HS), shape(3 * HS, C),
            shape(TOKENS, POOL * C), shape(4, TOKENS, TILE, dtype=BF16), shape(4, TOKENS, TILE, dtype=BF16),
        ),
        in_specs=[SMEM, VMEM, VMEM, ANY, ANY, ANY],
        out_specs=(VMEM,) * 4 + (ANY,) * 8,
        scratch_shapes=[
            pltpu.VMEM((POOL, WIN, C), F32),
            pltpu.VMEM((256, POOL * C), BF16),
            pltpu.VMEM((TOKENS + 16, 256), F32),
            pltpu.VMEM((3, C, 128), F32),
            pltpu.VMEM((TOKENS, C), F32),
            pltpu.VMEM((TOKENS, C), BF16),
            pltpu.VMEM((TOKENS, C), BF16),
            pltpu.VMEM((TOKENS, 128), F32),
            pltpu.VMEM((TOKENS, 3 * HS), F32),
            pltpu.VMEM((3 * HS, C), F32),
            pltpu.VMEM((TOKENS, POOL * C), F32),
            pltpu.VMEM((4, TOKENS, TILE), BF16),
            pltpu.VMEM((4, TOKENS, TILE), BF16),
            pltpu.SemaphoreType.DMA((3,)),
            pltpu.SemaphoreType.DMA((4,)),
            pltpu.SemaphoreType.DMA((2, 4)),
            pltpu.SemaphoreType.DMA((5,)),
        ],
        compiler_params=params(),
        name="attend",
    )


def decode():
    return pl.pallas_call(
        decode_kernel,
        out_shape=(shape(OWN, TRACKS), shape(HD, 128), shape(2 * OWN, C), shape(GROUP, 240, 128)),
        in_specs=[SMEM] + [VMEM] * 6,
        out_specs=(VMEM,) * 3 + (ANY,),
        scratch_shapes=[pltpu.VMEM((2 * OWN, C), F32), pltpu.VMEM((GROUP, 240, 128), F32), pltpu.SemaphoreType.DMA],
        compiler_params=params(),
        name="decode",
    )


def attend_back():
    return pl.pallas_call(
        attend_back_kernel,
        out_shape=shape(GROUP, 96, 128),
        in_specs=[SMEM] + [VMEM] * 7 + [ANY] * 5,
        out_specs=VMEM,
        scratch_shapes=[
            pltpu.VMEM((4, TOKENS, TILE), BF16),
            pltpu.VMEM((4, TOKENS, TILE), BF16),
            pltpu.VMEM((TOKENS, C), BF16),
            pltpu.VMEM((TOKENS, C), BF16),
            pltpu.VMEM((TOKENS, POOL * C), F32),
            pltpu.VMEM((TOKENS, HS), F32),
            pltpu.VMEM((3 * HS, TOKENS), F32),
            pltpu.VMEM((TOKENS, HS), F32),
            pltpu.VMEM((TOKENS, HS), F32),
            pltpu.VMEM((TOKENS, C), F32),
            pltpu.VMEM((POOL, 128, C), F32),
            pltpu.VMEM((128, C), F32),
            pltpu.SemaphoreType.DMA((6,)),
            pltpu.SemaphoreType.DMA((2, 4)),
        ],
        compiler_params=params(),
        name="attend_back",
    )


def finish():
    return pl.pallas_call(
        finish_kernel,
        out_shape=(shape(48, 4 * KW), shape(48, HD), shape(48, HD), shape(48, HD), shape(32, C), shape(48, TRACKS)),
        in_specs=[VMEM] * 2,
        out_specs=(VMEM,) * 6,
        compiler_params=params(),
        name="finish",
    )


def per_device(bases, targets, w_conv, w_query, w_key, w_value, w_out, w_head):
    s = lax.axis_index("seq")
    info = jnp.stack([lax.div(s, GROUP), lax.rem(s, GROUP)]).astype(jnp.int32)
    groups = [list(range(GROUP)), list(range(GROUP, 2 * GROUP))]

    def exchange(value):
        return lax.all_to_all(value, "seq", 0, 0, axis_index_groups=groups, tiled=True)

    targets_there = lax.ppermute(targets, "seq", [(i, i ^ GROUP) for i in range(2 * GROUP)])
    every = lax.all_to_all(jnp.broadcast_to(bases.reshape(1, 2, 128), (16, 2, 128)), "seq", 0, 0, tiled=True)

    x_own, hot_t, inverse, o_here, xh, xl, scales, qkv, w_t, slopes, eh, el = attend()(info, every, w_conv, w_query, w_key, w_value)
    log_rate, do_sent, dy, grads = decode()(info, exchange(o_here), x_own, targets, targets_there, w_out, w_head)
    grads = exchange(grads)
    sent = attend_back()(info, exchange(do_sent), qkv, inverse, w_t, hot_t, scales, dy, eh, el, xh, xl, slopes)
    sent, grads = lax.optimization_barrier((sent, grads))
    d_conv, d_query, d_key, d_value, d_out, d_head = finish()(exchange(sent), grads)
    return (log_rate, jnp.transpose(d_conv), d_query, d_key, d_value, d_out, d_head)


def solution(mesh):
    rows = P(("dp", "seq"), None)
    return jax.shard_map(
        per_device,
        mesh=mesh,
        in_specs=(P(("dp", "seq")), rows, P(), P(), P(), P(), P(), P()),
        out_specs=(rows, P("dp", "seq"), rows, rows, rows, rows, rows),
        check_vma=False,
    )
```

```python
import math

import jax
import jax.numpy as jnp
from jax import lax
from jax.experimental import pallas as pl
from jax.experimental.pallas import tpu as pltpu
from jax.sharding import PartitionSpec as P


C = 768
KW = 15
HEADS = 8
HS = 64
TRACKS = 128
POOL = 4
HD = 512
TOKENS = 1024
GROUP = 8
OWN = 64
F32 = jnp.float32
BF16 = jnp.bfloat16
GELU_A = math.sqrt(2.0 / math.pi)
GELU_C = 0.044715 / GELU_A ** 2
WIN = 80
TILE = 256

VMEM = pl.BlockSpec(memory_space=pltpu.VMEM)
SMEM = pl.BlockSpec(memory_space=pltpu.SMEM)
ANY = pl.BlockSpec(memory_space=pl.ANY)


def dot(left, right):
    return lax.dot_general(left, right, (((1,), (0,)), ((), ())), preferred_element_type=F32)


def split2(a):
    hi = a.astype(BF16)
    return hi, (a - hi.astype(F32)).astype(BF16)


def split3(a):
    hi = a.astype(BF16)
    rest = a - hi.astype(F32)
    mid = rest.astype(BF16)
    return hi, mid, (rest - mid.astype(F32)).astype(BF16)


def dot3(left, right):
    lh, ll = split2(left)
    rh, rl = split2(right)
    return dot(lh, rh) + (dot(lh, rl) + dot(ll, rh))


def dot3_narrow(left, right):
    lh, ll = split2(left)
    rh, rl = split2(right)
    n = right.shape[1]
    both = dot(lh, jnp.concatenate([rh, rl], axis=1))
    return both[:, :n] + (both[:, n:] + dot(ll, rh))


def dot3_short(left, right):
    lh, ll = split2(left)
    rh, rl = split2(right)
    n = left.shape[0]
    both = dot(jnp.concatenate([lh, ll], axis=0), rh)
    return both[:n] + (both[n:] + dot(lh, rl))


def dot3_thin(left, right):
    lh, ll = split2(left)
    rh, rl = split2(right)
    return dot(jnp.concatenate([lh, lh, ll], axis=1), jnp.concatenate([rh, rl, rh], axis=0))


def dot6(left, right):
    lh, lm, ll = split3(left)
    rh, rm, rl = split3(right)
    return dot(lh, rh) + ((dot(lh, rm) + dot(lm, rh)) + (dot(lm, rm) + (dot(lh, rl) + dot(ll, rh))))


def rms_scale(a):
    return lax.rsqrt(jnp.mean(a * a, axis=-1, keepdims=True) + 1e-06)


def conv_weights(w_ref, pad_ref, out_ref):
    pad_ref[...] = jnp.zeros_like(pad_ref)
    for r in range(POOL):
        pad_ref[r, 4 * (r + 1):4 * (r + 1) + 4 * KW, :] = w_ref[...] * GELU_A
    for r in range(POOL):
        pieces = split3(pad_ref[r])
        zeros = jnp.zeros((256 - 3 * WIN, C), BF16)
        out_ref[:, r * C:(r + 1) * C] = jnp.concatenate([*pieces, zeros], axis=0)


def key_stack(k):
    h, m, l = split3(k)
    return jnp.concatenate([h, m, l, h, m, h], axis=1)


def query_stack(q_t):
    h, m, l = split3(q_t)
    return jnp.concatenate([h, h, h, m, m, l], axis=0)


def attend_kernel(
    info, bases, w_conv, wq_hbm, wk_hbm, wv_hbm,
    x_own, hot_t, inverse, o_out, xh_hbm, xl_hbm, scale_hbm, qkv_hbm, w_t_hbm, slopes_hbm, eh_hbm, el_hbm,
    pad, w_all, window, slabs, x_all, xh_out, xl_out, scale_out, qkv_out, w_t, slopes, eh_all, el_all, sems, slope_sems, e_sems, out_sems, chunk_sems,
):
    half, m = info[0], info[1]
    copies = []
    for i, w in enumerate((wq_hbm, wk_hbm, wv_hbm)):
        lanes = pl.ds(pl.multiple_of(lax.div(m, 2) * 128, 128), 128)
        copies.append(pltpu.make_async_copy(w.at[:, lanes], slabs.at[i], sems.at[i]))
    for copy in copies:
        copy.start()
    conv_weights(w_conv, pad, w_all)

    lane = lax.broadcasted_iota(jnp.int32, (128, 256), 1)
    row = lax.broadcasted_iota(jnp.int32, (128, 256), 0)
    within = lax.rem(lane, WIN)
    place = lax.div(lax.rem(within, 16), 4)
    pick = jnp.where(lax.rem(row, 4) == place, 1.0, 0.0).astype(BF16)
    mine = lax.broadcasted_iota(jnp.int32, (32, 128), 0) == lax.div(lax.broadcasted_iota(jnp.int32, (32, 128), 1), 4)
    code = lax.rem(lax.broadcasted_iota(jnp.int32, (1, 256), 1), 4).astype(F32)
    window[0:8, :] = jnp.zeros((8, 256), F32)
    window[TOKENS + 8:TOKENS + 16, :] = jnp.zeros((8, 256), F32)
    for part in range(8):
        pieces = []
        for q in range(4 * part, 4 * part + 4):
            line = bases[q // 2, q % 2:q % 2 + 1, :].astype(F32)
            pieces.append(jnp.where(mine, jnp.broadcast_to(line, (32, 128)), 0.0))
        value = dot(jnp.concatenate(pieces, axis=0).astype(BF16), pick)
        window[8 + 128 * part:8 + 128 * part + 128, :] = jnp.where(value == code, 1.0, 0.0)

    shift = lax.div(lax.rem(lax.broadcasted_iota(jnp.int32, (TILE, 256), 1), WIN), 16)
    real = lax.broadcasted_iota(jnp.int32, (TILE, 256), 1) < 3 * WIN
    steps = TOKENS // TILE

    def encode(c, _):
        start = pl.multiple_of(lax.rem(c + half * (steps // 2), steps) * TILE, TILE)
        around = window[pl.ds(start, TILE + 16), :]
        hot = jnp.zeros((TILE, 256), F32)
        for d in range(5):
            hot = jnp.where(shift == d, around[6 + d:6 + d + TILE, :], hot)
        hot = jnp.where(real, hot, 0.0).astype(BF16)
        here = pl.ds(pl.multiple_of(c * TILE, TILE), TILE)
        total = None
        for r in range(POOL):
            y = dot(hot, w_all[:, r * C:(r + 1) * C])
            cube = y * (y * y * GELU_C)
            t = jnp.tanh(y + cube)
            up = 1.0 + t
            total = y * up if total is None else total + y * up
            slopes[here, r * C:(r + 1) * C] = up + (1.0 - t * t) * (y + 3.0 * cube)
        x_all[here, :] = total * (0.5 / (GELU_A * POOL))
        hot_t[:, here] = jnp.transpose(hot[:, :128].astype(F32)).astype(BF16)
        pltpu.make_async_copy(slopes.at[here], slopes_hbm.at[here], slope_sems.at[c]).start()
        return 0

    for copy in copies:
        copy.wait()
    odd = lax.rem(m, 2) == 1
    columns = [jnp.where(odd, slabs[i, :, HS:], slabs[i, :, :HS]) for i in range(3)]
    w_t[...] = jnp.transpose(jnp.concatenate(columns, axis=1))
    w_qkv = jnp.concatenate([columns[0] * HS ** -0.5, columns[1], columns[2]], axis=1)
    wh, wm, wl = split3(w_qkv)

    chunked = ((xh_out, xh_hbm), (xl_out, xl_hbm), (scale_out, scale_hbm))

    def project(c, _):
        here = pl.ds(pl.multiple_of(c * TILE, TILE), TILE)
        x = x_all[here, :]
        scale = rms_scale(x)
        scale_out[here, :] = jnp.broadcast_to(scale, (TILE, 128))
        xn = x * scale
        h, mid, low = split3(xn)
        xh_out[here, :] = h
        xl_out[here, :] = mid
        for i, (a, b) in enumerate(chunked):
            pltpu.make_async_copy(a.at[here], b.at[here], chunk_sems.at[i, c]).start()
        qkv_out[here, :] = dot(h, wh) + ((dot(h, wm) + dot(mid, wh)) + (dot(mid, wm) + (dot(h, wl) + dot(low, wh))))
        return 0

    encode(0, 0)

    def both_steps(c, _):
        project(c - 1, 0)
        encode(c, 0)
        return 0

    lax.fori_loop(1, steps, both_steps, 0)
    project(steps - 1, 0)
    for part in range(2):
        here = pl.ds(pl.multiple_of(part * 512 + m * OWN, OWN), OWN)
        x_own[part * OWN:(part + 1) * OWN, :] = x_all[here, :]

    outs_copies = [
        pltpu.make_async_copy(a, b, out_sems.at[i])
        for i, (a, b) in enumerate(((qkv_out, qkv_hbm), (w_t, w_t_hbm)))
    ]
    for copy in outs_copies:
        copy.start()
    qkv = qkv_out[...]
    q_t = query_stack(jnp.transpose(qkv[:, :HS]))
    keys = key_stack(qkv[:, HS:2 * HS])
    vh, vl = split2(jnp.transpose(qkv[:, 2 * HS:]))
    v_both = jnp.concatenate([vh, vl], axis=0)
    outs = []
    following = dot(keys, q_t[:, :TILE])
    for c in range(steps):
        scores = following
        if c + 1 < steps:
            following = dot(keys, q_t[:, (c + 1) * TILE:(c + 2) * TILE])
        e = jnp.exp(scores - jnp.max(scores, axis=0, keepdims=True))
        eh, el = split2(e)
        over = 1.0 / jnp.sum(eh.astype(F32) + el.astype(F32), axis=0, keepdims=True)
        inverse[:, c * TILE:(c + 1) * TILE] = over
        eh_all[c] = eh
        el_all[c] = el
        for i, (here, there) in enumerate(((eh_all, eh_hbm), (el_all, el_hbm))):
            pltpu.make_async_copy(here.at[c], there.at[c], e_sems.at[i, c]).start()
        both = dot(v_both, eh)
        outs.append(jnp.transpose((both[:HS] + (both[HS:] + dot(vh, el))) * over))
    o_out[...] = jnp.concatenate(
        [jnp.concatenate(outs[:steps // 2], axis=0), jnp.concatenate(outs[steps // 2:], axis=0)], axis=1
    )
    for copy in outs_copies:
        copy.wait()
    for c in range(steps):
        here = pl.ds(c * TILE, TILE)
        for i, (a, b) in enumerate(chunked):
            pltpu.make_async_copy(a.at[here], b.at[here], chunk_sems.at[i, c]).wait()
        pltpu.make_async_copy(slopes.at[here], slopes_hbm.at[here], slope_sems.at[c]).wait()
        pltpu.make_async_copy(eh_all.at[c], eh_hbm.at[c], e_sems.at[0, c]).wait()
        pltpu.make_async_copy(el_all.at[c], el_hbm.at[c], e_sems.at[1, c]).wait()


def decode_kernel(
    o_parts, x_own, targets_here, targets_there, w_out, w_head,
    log_rate, do_out, dy_out, yn_all, d_rate_out,
):
    parts = [o_parts[h * OWN:(h + 1) * OWN, :] for h in range(HEADS)]
    attended = jnp.concatenate(
        [jnp.concatenate([p[:, :HS] for p in parts], axis=1), jnp.concatenate([p[:, HS:] for p in parts], axis=1)], axis=0
    )
    wout = w_out[...]
    wouth, woutl = split2(wout)
    ah, al = split2(attended)
    both = dot(jnp.concatenate([ah, al], axis=0), wouth)
    y = x_own[...] + (both[:2 * OWN] + (both[2 * OWN:] + dot(ah, woutl)))
    scale = rms_scale(y)
    yn = y * scale
    yn_all[...] = yn
    rate = dot3_narrow(yn, w_head[...])
    log_rate[...] = rate[:OWN]
    targets = jnp.concatenate([targets_here[...], targets_there[...]], axis=0).astype(F32)
    d_rate = (jnp.exp(rate) - targets) * (1.0 / math.sqrt(TOKENS))
    d_rate_out[...] = d_rate
    d_yn = dot3_thin(d_rate, jnp.transpose(w_head[...]))
    dy = scale * (d_yn - yn * jnp.mean(d_yn * yn, axis=-1, keepdims=True))
    dy_out[...] = dy
    dth, dtl = split2(jnp.transpose(dy))
    both = dot(wouth, jnp.concatenate([dth, dtl], axis=1))
    do_out[...] = both[:, :2 * OWN] + (both[:, 2 * OWN:] + dot(woutl, dth))


def share_kernel(info, o_parts, dy, yn_all, d_rate_ref, grads_out):
    half = info[0]
    d_rate = d_rate_ref[...]
    heads = o_parts[pl.ds(pl.multiple_of(half * 256, 256), 256), :]
    o_t = jnp.concatenate(
        [
            jnp.concatenate(
                [jnp.transpose(heads[h * OWN:(h + 1) * OWN, :])[:HS], jnp.transpose(heads[h * OWN:(h + 1) * OWN, :])[HS:]], axis=1
            )
            for h in range(4)
        ],
        axis=0,
    )
    d_out = dot3_thin(o_t, dy[...])
    yn_half = yn_all[:, pl.ds(pl.multiple_of(half * 384, 128), 384)]
    d_head = dot3_thin(jnp.transpose(yn_half), d_rate)
    for p in range(GROUP):
        for j in range(6):
            grads_out[p, 32 * j:32 * j + 32, :] = d_out[32 * p:32 * p + 32, 128 * j:128 * j + 128]
        grads_out[p, 192:240, :] = d_head[48 * p:48 * p + 48, :]


def attend_back_kernel(
    info, do_parts, qkv_ref, inverse, w_t_hbm, hot_t_hbm, scales_hbm, dy_hbm, eh_hbm, el_hbm, xh_hbm, xl_hbm, slopes_hbm,
    sent,
    w_t, hot_t, scales, dy, eh_all, el_all, xh, xl, slopes, do_all, g_t, dk_acc, dv_acc, dy_all, conv_acc, dconv, sems, e_sems,
):
    half, m = info[0], info[1]
    steps = TOKENS // TILE
    e_copies = [
        [pltpu.make_async_copy(there.at[c], here.at[c], e_sems.at[i, c]) for i, (there, here) in enumerate(((eh_hbm, eh_all), (el_hbm, el_all)))]
        for c in range(steps)
    ]
    copies = [pltpu.make_async_copy(a, b, sems.at[i]) for i, (a, b) in enumerate(((dy_hbm, dy), (xh_hbm, xh), (xl_hbm, xl), (w_t_hbm, w_t), (hot_t_hbm, hot_t), (scales_hbm, scales)))]
    copies += [
        pltpu.make_async_copy(slopes_hbm.at[pl.ds(c * TILE, TILE)], slopes.at[pl.ds(c * TILE, TILE)], sems.at[6 + c]) for c in range(steps)
    ]
    for pair in e_copies:
        for copy in pair:
            copy.start()
    for copy in copies:
        copy.start()
    for p in range(GROUP):
        both = jnp.transpose(do_parts[p * OWN:(p + 1) * OWN, :])
        do_all[p * OWN:(p + 1) * OWN, :] = both[:OWN]
        do_all[512 + p * OWN:512 + (p + 1) * OWN, :] = both[OWN:]
    qkv = qkv_ref[...]
    kh, kl = split2(jnp.transpose(qkv[:, HS:2 * HS]))
    k_both = jnp.concatenate([kh, kl], axis=0)
    vh, vl = split2(qkv[:, 2 * HS:])
    v_three = jnp.concatenate([vh, vh, vl], axis=1)
    turned = jnp.transpose(do_all[...])
    dth, dtl = split2(turned)
    do_t = jnp.concatenate([dth, dtl, dth], axis=0)
    dh, dl = split2(jnp.transpose(turned * inverse[...]))
    do_both = jnp.concatenate([dh, dl], axis=1)
    qh, ql = split2(qkv[:, :HS])
    q_both = jnp.concatenate([qh, ql], axis=1)
    dy_all[...] = jnp.zeros_like(dy_all)
    following = dot(v_three, do_t[:, :TILE])
    for c in range(steps):
        here = slice(c * TILE, (c + 1) * TILE)
        dp = following
        if c + 1 < steps:
            following = dot(v_three, do_t[:, (c + 1) * TILE:(c + 2) * TILE])
        for copy in e_copies[c]:
            copy.wait()
        eh, el = eh_all[c], el_all[c]
        p = (eh.astype(F32) + el.astype(F32)) * inverse[:, here]
        ds = p * (dp - jnp.sum(p * dp, axis=0, keepdims=True))
        sh, sl = split2(ds)
        both = dot(k_both, sh)
        g_t[0:HS, here] = (both[:HS] + (both[HS:] + dot(kh, sl))) * (HS ** -0.5)
        both = dot(eh, do_both[here])
        dv = both[:, :HS] + (both[:, HS:] + dot(el, dh[here]))
        both = dot(sh, q_both[here])
        dk = both[:, :HS] + (both[:, HS:] + dot(sl, qh[here]))
        if c == 0:
            dk_acc[...] = dk
            dv_acc[...] = dv
        else:
            dk_acc[...] += dk
            dv_acc[...] += dv
    g_t[HS:2 * HS, :] = jnp.transpose(dk_acc[...])
    g_t[2 * HS:3 * HS, :] = jnp.transpose(dv_acc[...])
    for copy in copies[:6]:
        copy.wait()
    for part in range(2):
        dy_all[pl.ds(pl.multiple_of(part * 512 + m * OWN, OWN), OWN), :] = dy[part * OWN:(part + 1) * OWN, :]
    lanes = pl.ds(pl.multiple_of(half * 384, 128), 384)
    gh, gl = split2(g_t[...])
    both = dot(jnp.concatenate([gh, gl], axis=0), xh[:, lanes])
    d_w = jnp.transpose(both[:192] + (both[192:] + dot(gh, xl[:, lanes])))

    wh, wl = split2(w_t[...])
    w_three = jnp.concatenate([wh, wl, wh], axis=0)

    def back_to_xn(c):
        gh, gl = split2(jnp.transpose(g_t[:, c * TILE:(c + 1) * TILE]))
        return dot(jnp.concatenate([gh, gh, gl], axis=1), w_three)

    following = back_to_xn(0)
    for c in range(steps):
        here = slice(c * TILE, (c + 1) * TILE)
        d_xn = following
        if c + 1 < steps:
            following = back_to_xn(c + 1)
        xn = xh[here].astype(F32) + xl[here].astype(F32)
        mean = jnp.mean(d_xn * xn, axis=-1, keepdims=True)
        d_x = (dy_all[here] + scales[here, :1] * (d_xn - xn * mean)) * (0.5 / POOL)
        copies[6 + c].wait()
        hot = hot_t[:, here]
        for r in range(POOL):
            dh, dl = split2(d_x * slopes[here, r * C:(r + 1) * C])
            moved = dot(hot, dh) + dot(hot, dl)
            if c == 0:
                conv_acc[r] = moved
            else:
                conv_acc[r] += moved
    summed = conv_acc[0, 4:4 + 4 * KW, :]
    for r in range(1, POOL):
        summed += conv_acc[r, 4 * (r + 1):4 * (r + 1) + 4 * KW, :]
    dconv[...] = jnp.zeros_like(dconv)
    dconv[0:4 * KW, :] = summed
    d_conv = jnp.transpose(dconv[:, lanes])
    for p in range(GROUP):
        mine = d_w[48 * p:48 * p + 48, :]
        sent[p, 0:48, :] = mine[:, :128]
        sent[p, 48:72, :] = jnp.concatenate([mine[:24, 128:], mine[24:, 128:]], axis=1)
        mine = d_conv[48 * p:48 * p + 48, :HS]
        sent[p, 72:96, :] = jnp.concatenate([mine[:24], mine[24:]], axis=1)


def sum_kernel(grads, d_out, d_head):
    every = grads[0]
    for p in range(1, GROUP):
        every = every + grads[p]
    d_out[...] = jnp.concatenate([every[32 * j:32 * j + 32, :] for j in range(6)], axis=1)
    d_head[...] = every[192:240, :]


def finish_kernel(got, d_conv, d_query, d_key, d_value):
    total = got[0, 72:96, :]
    for p in range(1, GROUP):
        total = total + got[p, 72:96, :]
    d_conv[...] = jnp.concatenate([total[:, :HS], total[:, HS:]], axis=0)[:, :4 * KW]
    for part, out in enumerate((d_query, d_key)):
        out[...] = jnp.concatenate([got[h, 0:48, part * HS:(part + 1) * HS] for h in range(HEADS)], axis=1)
    rows = [got[h, 48:72, :] for h in range(HEADS)]
    d_value[...] = jnp.concatenate([jnp.concatenate([r[:, :HS], r[:, HS:]], axis=0) for r in rows], axis=1)


def shape(*dims, dtype=F32):
    return jax.ShapeDtypeStruct(dims, dtype)


def params(mib=60):
    return pltpu.CompilerParams(vmem_limit_bytes=mib * 1024 * 1024)


def attend():
    return pl.pallas_call(
        attend_kernel,
        out_shape=(
            shape(2 * OWN, C), shape(128, TOKENS, dtype=BF16), shape(1, TOKENS), shape(512, 128),
            shape(TOKENS, C, dtype=BF16), shape(TOKENS, C, dtype=BF16), shape(TOKENS, 128), shape(TOKENS, 3 * HS), shape(3 * HS, C),
            shape(TOKENS, POOL * C), shape(4, TOKENS, TILE, dtype=BF16), shape(4, TOKENS, TILE, dtype=BF16),
        ),
        in_specs=[SMEM, VMEM, VMEM, ANY, ANY, ANY],
        out_specs=(VMEM,) * 4 + (ANY,) * 8,
        scratch_shapes=[
            pltpu.VMEM((POOL, WIN, C), F32),
            pltpu.VMEM((256, POOL * C), BF16),
            pltpu.VMEM((TOKENS + 16, 256), F32),
            pltpu.VMEM((3, C, 128), F32),
            pltpu.VMEM((TOKENS, C), F32),
            pltpu.VMEM((TOKENS, C), BF16),
            pltpu.VMEM((TOKENS, C), BF16),
            pltpu.VMEM((TOKENS, 128), F32),
            pltpu.VMEM((TOKENS, 3 * HS), F32),
            pltpu.VMEM((3 * HS, C), F32),
            pltpu.VMEM((TOKENS, POOL * C), F32),
            pltpu.VMEM((4, TOKENS, TILE), BF16),
            pltpu.VMEM((4, TOKENS, TILE), BF16),
            pltpu.SemaphoreType.DMA((3,)),
            pltpu.SemaphoreType.DMA((4,)),
            pltpu.SemaphoreType.DMA((2, 4)),
            pltpu.SemaphoreType.DMA((2,)),
            pltpu.SemaphoreType.DMA((3, 4)),
        ],
        compiler_params=params(),
        name="attend",
    )


def decode():
    return pl.pallas_call(
        decode_kernel,
        out_shape=(shape(OWN, TRACKS), shape(HD, 128), shape(2 * OWN, C), shape(2 * OWN, C), shape(2 * OWN, TRACKS)),
        in_specs=[VMEM] * 6,
        out_specs=(VMEM,) * 5,
        compiler_params=params(16),
        name="decode",
    )


def share():
    return pl.pallas_call(
        share_kernel,
        out_shape=shape(GROUP, 240, 128),
        in_specs=[SMEM] + [VMEM] * 4,
        out_specs=VMEM,
        compiler_params=params(16),
        name="share",
    )


def attend_back():
    return pl.pallas_call(
        attend_back_kernel,
        out_shape=shape(GROUP, 96, 128),
        in_specs=[SMEM] + [VMEM] * 3 + [ANY] * 9,
        out_specs=VMEM,
        scratch_shapes=[
            pltpu.VMEM((3 * HS, C), F32),
            pltpu.VMEM((128, TOKENS), BF16),
            pltpu.VMEM((TOKENS, 128), F32),
            pltpu.VMEM((2 * OWN, C), F32),
            pltpu.VMEM((4, TOKENS, TILE), BF16),
            pltpu.VMEM((4, TOKENS, TILE), BF16),
            pltpu.VMEM((TOKENS, C), BF16),
            pltpu.VMEM((TOKENS, C), BF16),
            pltpu.VMEM((TOKENS, POOL * C), F32),
            pltpu.VMEM((TOKENS, HS), F32),
            pltpu.VMEM((3 * HS, TOKENS), F32),
            pltpu.VMEM((TOKENS, HS), F32),
            pltpu.VMEM((TOKENS, HS), F32),
            pltpu.VMEM((TOKENS, C), F32),
            pltpu.VMEM((POOL, 128, C), F32),
            pltpu.VMEM((128, C), F32),
            pltpu.SemaphoreType.DMA((10,)),
            pltpu.SemaphoreType.DMA((2, 4)),
        ],
        compiler_params=params(),
        name="attend_back",
    )


def add_up():
    return pl.pallas_call(
        sum_kernel,
        out_shape=(shape(32, C), shape(48, TRACKS)),
        in_specs=[VMEM],
        out_specs=(VMEM,) * 2,
        compiler_params=params(8),
        name="add_up",
    )


def finish():
    return pl.pallas_call(
        finish_kernel,
        out_shape=(shape(48, 4 * KW), shape(48, HD), shape(48, HD), shape(48, HD)),
        in_specs=[VMEM],
        out_specs=(VMEM,) * 4,
        compiler_params=params(8),
        name="finish",
    )


def per_device(bases, targets, w_conv, w_query, w_key, w_value, w_out, w_head):
    s = lax.axis_index("seq")
    info = jnp.stack([lax.div(s, GROUP), lax.rem(s, GROUP)]).astype(jnp.int32)
    groups = [list(range(GROUP)), list(range(GROUP, 2 * GROUP))]

    def exchange(value):
        return lax.all_to_all(value, "seq", 0, 0, axis_index_groups=groups, tiled=True)

    targets_there = lax.ppermute(targets, "seq", [(i, i ^ GROUP) for i in range(2 * GROUP)])
    every = lax.all_to_all(jnp.broadcast_to(bases.reshape(1, 2, 128), (16, 2, 128)), "seq", 0, 0, tiled=True)

    every, targets_there = lax.optimization_barrier((every, targets_there))
    x_own, hot_t, inverse, o_here, xh, xl, scales, qkv, w_t, slopes, eh, el = attend()(info, every, w_conv, w_query, w_key, w_value)
    o_parts = exchange(o_here)
    log_rate, do_sent, dy, yn, d_rate = decode()(o_parts, x_own, targets, targets_there, w_out, w_head)
    do_parts = exchange(do_sent)
    grads = exchange(share()(info, o_parts, dy, yn, d_rate))
    sent = attend_back()(info, do_parts, qkv, inverse, w_t, hot_t, scales, dy, eh, el, xh, xl, slopes)
    sent, grads = lax.optimization_barrier((sent, grads))
    d_out, d_head = add_up()(grads)
    d_conv, d_query, d_key, d_value = finish()(exchange(sent))
    return (log_rate, jnp.transpose(d_conv), d_query, d_key, d_value, d_out, d_head)


def solution(mesh):
    rows = P(("dp", "seq"), None)
    return jax.shard_map(
        per_device,
        mesh=mesh,
        in_specs=(P(("dp", "seq")), rows, P(), P(), P(), P(), P(), P()),
        out_specs=(rows, P("dp", "seq"), rows, rows, rows, rows, rows),
        check_vma=False,
    )
```

```python
import math

import jax
import jax.numpy as jnp
from jax import lax
from jax.experimental import pallas as pl
from jax.experimental.pallas import tpu as pltpu
from jax.sharding import PartitionSpec as P


C = 768
KW = 15
HEADS = 8
HS = 64
TRACKS = 128
POOL = 4
HD = 512
TOKENS = 1024
GROUP = 8
OWN = 64
F32 = jnp.float32
BF16 = jnp.bfloat16
GELU_A = math.sqrt(2.0 / math.pi)
GELU_C = 0.044715 / GELU_A ** 2
WIN = 80
TILE = 256

VMEM = pl.BlockSpec(memory_space=pltpu.VMEM)
SMEM = pl.BlockSpec(memory_space=pltpu.SMEM)
ANY = pl.BlockSpec(memory_space=pl.ANY)


def dot(left, right):
    return lax.dot_general(left, right, (((1,), (0,)), ((), ())), preferred_element_type=F32)


def split2(a):
    hi = a.astype(BF16)
    return hi, (a - hi.astype(F32)).astype(BF16)


def split3(a):
    hi = a.astype(BF16)
    rest = a - hi.astype(F32)
    mid = rest.astype(BF16)
    return hi, mid, (rest - mid.astype(F32)).astype(BF16)


def dot3(left, right):
    lh, ll = split2(left)
    rh, rl = split2(right)
    return dot(lh, rh) + (dot(lh, rl) + dot(ll, rh))


def dot3_narrow(left, right):
    lh, ll = split2(left)
    rh, rl = split2(right)
    n = right.shape[1]
    both = dot(lh, jnp.concatenate([rh, rl], axis=1))
    return both[:, :n] + (both[:, n:] + dot(ll, rh))


def dot3_short(left, right):
    lh, ll = split2(left)
    rh, rl = split2(right)
    n = left.shape[0]
    both = dot(jnp.concatenate([lh, ll], axis=0), rh)
    return both[:n] + (both[n:] + dot(lh, rl))


def dot3_thin(left, right):
    lh, ll = split2(left)
    rh, rl = split2(right)
    return dot(jnp.concatenate([lh, lh, ll], axis=1), jnp.concatenate([rh, rl, rh], axis=0))


def dot6(left, right):
    lh, lm, ll = split3(left)
    rh, rm, rl = split3(right)
    return dot(lh, rh) + ((dot(lh, rm) + dot(lm, rh)) + (dot(lm, rm) + (dot(lh, rl) + dot(ll, rh))))


def rms_scale(a):
    return lax.rsqrt(jnp.mean(a * a, axis=-1, keepdims=True) + 1e-06)


def conv_weights(w_ref, pad_ref, out_ref):
    pad_ref[...] = jnp.zeros_like(pad_ref)
    for r in range(POOL):
        pad_ref[r, 4 * (r + 1):4 * (r + 1) + 4 * KW, :] = w_ref[...] * GELU_A
    for r in range(POOL):
        pieces = split3(pad_ref[r])
        zeros = jnp.zeros((256 - 3 * WIN, C), BF16)
        out_ref[:, r * C:(r + 1) * C] = jnp.concatenate([*pieces, zeros], axis=0)


def key_stack(k):
    h, m, l = split3(k)
    return jnp.concatenate([h, m, l, h, m, h], axis=1)


def query_stack(q_t):
    h, m, l = split3(q_t)
    return jnp.concatenate([h, h, h, m, m, l], axis=0)


def attend_kernel(
    info, bases, w_conv, wq_hbm, wk_hbm, wv_hbm,
    x_own, hot_t, inverse, o_out, xh_hbm, xl_hbm, scale_hbm, qkv_hbm, w_t_hbm, slopes_hbm, eh_hbm, el_hbm,
    pad, w_all, window, slabs, x_all, xh_out, xl_out, scale_out, qkv_out, w_t, slopes, eh_all, el_all, sems, slope_sems, e_sems, out_sems, chunk_sems,
):
    half, m = info[0], info[1]
    copies = []
    for i, w in enumerate((wq_hbm, wk_hbm, wv_hbm)):
        lanes = pl.ds(pl.multiple_of(lax.div(m, 2) * 128, 128), 128)
        copies.append(pltpu.make_async_copy(w.at[:, lanes], slabs.at[i], sems.at[i]))
    for copy in copies:
        copy.start()
    conv_weights(w_conv, pad, w_all)

    lane = lax.broadcasted_iota(jnp.int32, (128, 256), 1)
    row = lax.broadcasted_iota(jnp.int32, (128, 256), 0)
    within = lax.rem(lane, WIN)
    place = lax.div(lax.rem(within, 16), 4)
    pick = jnp.where(lax.rem(row, 4) == place, 1.0, 0.0).astype(BF16)
    mine = lax.broadcasted_iota(jnp.int32, (32, 128), 0) == lax.div(lax.broadcasted_iota(jnp.int32, (32, 128), 1), 4)
    code = lax.rem(lax.broadcasted_iota(jnp.int32, (1, 256), 1), 4).astype(F32)
    window[0:8, :] = jnp.zeros((8, 256), F32)
    window[TOKENS + 8:TOKENS + 16, :] = jnp.zeros((8, 256), F32)
    for part in range(8):
        pieces = []
        for q in range(4 * part, 4 * part + 4):
            line = bases[q // 2, q % 2:q % 2 + 1, :].astype(F32)
            pieces.append(jnp.where(mine, jnp.broadcast_to(line, (32, 128)), 0.0))
        value = dot(jnp.concatenate(pieces, axis=0).astype(BF16), pick)
        window[8 + 128 * part:8 + 128 * part + 128, :] = jnp.where(value == code, 1.0, 0.0)

    shift = lax.div(lax.rem(lax.broadcasted_iota(jnp.int32, (TILE, 256), 1), WIN), 16)
    real = lax.broadcasted_iota(jnp.int32, (TILE, 256), 1) < 3 * WIN
    steps = TOKENS // TILE

    def encode(c, _):
        start = pl.multiple_of(lax.rem(c + half * (steps // 2), steps) * TILE, TILE)
        around = window[pl.ds(start, TILE + 16), :]
        hot = jnp.zeros((TILE, 256), F32)
        for d in range(5):
            hot = jnp.where(shift == d, around[6 + d:6 + d + TILE, :], hot)
        hot = jnp.where(real, hot, 0.0).astype(BF16)
        here = pl.ds(pl.multiple_of(c * TILE, TILE), TILE)
        total = None
        for r in range(POOL):
            y = dot(hot, w_all[:, r * C:(r + 1) * C])
            cube = y * (y * y * GELU_C)
            t = jnp.tanh(y + cube)
            up = 1.0 + t
            total = y * up if total is None else total + y * up
            slopes[here, r * C:(r + 1) * C] = up + (1.0 - t * t) * (y + 3.0 * cube)
        x_all[here, :] = total * (0.5 / (GELU_A * POOL))
        hot_t[:, here] = jnp.transpose(hot[:, :128].astype(F32)).astype(BF16)
        pltpu.make_async_copy(slopes.at[here], slopes_hbm.at[here], slope_sems.at[c]).start()
        return 0

    for copy in copies:
        copy.wait()
    odd = lax.rem(m, 2) == 1
    columns = [jnp.where(odd, slabs[i, :, HS:], slabs[i, :, :HS]) for i in range(3)]
    w_t[...] = jnp.transpose(jnp.concatenate(columns, axis=1))
    w_qkv = jnp.concatenate([columns[0] * HS ** -0.5, columns[1], columns[2]], axis=1)
    wh, wm, wl = split3(w_qkv)

    chunked = ((xh_out, xh_hbm), (xl_out, xl_hbm), (scale_out, scale_hbm))

    def project(c, _):
        here = pl.ds(pl.multiple_of(c * TILE, TILE), TILE)
        x = x_all[here, :]
        scale = rms_scale(x)
        scale_out[here, :] = jnp.broadcast_to(scale, (TILE, 128))
        xn = x * scale
        h, mid, low = split3(xn)
        xh_out[here, :] = h
        xl_out[here, :] = mid
        for i, (a, b) in enumerate(chunked):
            pltpu.make_async_copy(a.at[here], b.at[here], chunk_sems.at[i, c]).start()
        qkv_out[here, :] = dot(h, wh) + ((dot(h, wm) + dot(mid, wh)) + (dot(mid, wm) + (dot(h, wl) + dot(low, wh))))
        return 0

    encode(0, 0)

    def both_steps(c, _):
        project(c - 1, 0)
        encode(c, 0)
        return 0

    lax.fori_loop(1, steps, both_steps, 0)
    project(steps - 1, 0)
    for part in range(2):
        here = pl.ds(pl.multiple_of(part * 512 + m * OWN, OWN), OWN)
        x_own[part * OWN:(part + 1) * OWN, :] = x_all[here, :]

    outs_copies = [
        pltpu.make_async_copy(a, b, out_sems.at[i])
        for i, (a, b) in enumerate(((qkv_out, qkv_hbm), (w_t, w_t_hbm)))
    ]
    for copy in outs_copies:
        copy.start()
    qkv = qkv_out[...]
    q_t = query_stack(jnp.transpose(qkv[:, :HS]))
    keys = key_stack(qkv[:, HS:2 * HS])
    vh, vl = split2(jnp.transpose(qkv[:, 2 * HS:]))
    v_both = jnp.concatenate([vh, vl], axis=0)
    outs = []
    following = dot(keys, q_t[:, :TILE])
    for c in range(steps):
        scores = following
        if c + 1 < steps:
            following = dot(keys, q_t[:, (c + 1) * TILE:(c + 2) * TILE])
        e = jnp.exp(scores - jnp.max(scores, axis=0, keepdims=True))
        eh, el = split2(e)
        over = 1.0 / jnp.sum(eh.astype(F32) + el.astype(F32), axis=0, keepdims=True)
        inverse[:, c * TILE:(c + 1) * TILE] = over
        eh_all[c] = eh
        el_all[c] = el
        for i, (here, there) in enumerate(((eh_all, eh_hbm), (el_all, el_hbm))):
            pltpu.make_async_copy(here.at[c], there.at[c], e_sems.at[i, c]).start()
        both = dot(v_both, eh)
        outs.append(jnp.transpose((both[:HS] + (both[HS:] + dot(vh, el))) * over))
    o_out[...] = jnp.concatenate(
        [jnp.concatenate(outs[:steps // 2], axis=0), jnp.concatenate(outs[steps // 2:], axis=0)], axis=1
    )
    for copy in outs_copies:
        copy.wait()
    for c in range(steps):
        here = pl.ds(c * TILE, TILE)
        for i, (a, b) in enumerate(chunked):
            pltpu.make_async_copy(a.at[here], b.at[here], chunk_sems.at[i, c]).wait()
        pltpu.make_async_copy(slopes.at[here], slopes_hbm.at[here], slope_sems.at[c]).wait()
        pltpu.make_async_copy(eh_all.at[c], eh_hbm.at[c], e_sems.at[0, c]).wait()
        pltpu.make_async_copy(el_all.at[c], el_hbm.at[c], e_sems.at[1, c]).wait()


def decode_kernel(
    o_parts, x_own, targets_here, targets_there, w_out, w_head,
    log_rate, do_out, dy_out, yn_all, d_rate_out,
):
    parts = [o_parts[h * OWN:(h + 1) * OWN, :] for h in range(HEADS)]
    attended = jnp.concatenate(
        [jnp.concatenate([p[:, :HS] for p in parts], axis=1), jnp.concatenate([p[:, HS:] for p in parts], axis=1)], axis=0
    )
    wout = w_out[...]
    wouth, woutl = split2(wout)
    ah, al = split2(attended)
    both = dot(jnp.concatenate([ah, al], axis=0), wouth)
    y = x_own[...] + (both[:2 * OWN] + (both[2 * OWN:] + dot(ah, woutl)))
    scale = rms_scale(y)
    yn = y * scale
    yn_all[...] = yn
    rate = dot3_narrow(yn, w_head[...])
    log_rate[...] = rate[:OWN]
    targets = jnp.concatenate([targets_here[...], targets_there[...]], axis=0).astype(F32)
    d_rate = (jnp.exp(rate) - targets) * (1.0 / math.sqrt(TOKENS))
    d_rate_out[...] = d_rate
    d_yn = dot3_thin(d_rate, jnp.transpose(w_head[...]))
    dy = scale * (d_yn - yn * jnp.mean(d_yn * yn, axis=-1, keepdims=True))
    dy_out[...] = dy
    dth, dtl = split2(jnp.transpose(dy))
    both = dot(wouth, jnp.concatenate([dth, dtl], axis=1))
    do_out[...] = both[:, :2 * OWN] + (both[:, 2 * OWN:] + dot(woutl, dth))


def share_kernel(info, o_parts, dy, yn_all, d_rate_ref, grads_out):
    half = info[0]
    d_rate = d_rate_ref[...]
    heads = o_parts[pl.ds(pl.multiple_of(half * 256, 256), 256), :]
    o_t = jnp.concatenate(
        [
            jnp.concatenate(
                [jnp.transpose(heads[h * OWN:(h + 1) * OWN, :])[:HS], jnp.transpose(heads[h * OWN:(h + 1) * OWN, :])[HS:]], axis=1
            )
            for h in range(4)
        ],
        axis=0,
    )
    d_out = dot3_thin(o_t, dy[...])
    yn_half = yn_all[:, pl.ds(pl.multiple_of(half * 384, 128), 384)]
    d_head = dot3_thin(jnp.transpose(yn_half), d_rate)
    for p in range(GROUP):
        for j in range(6):
            grads_out[p, 32 * j:32 * j + 32, :] = d_out[32 * p:32 * p + 32, 128 * j:128 * j + 128]
        grads_out[p, 192:240, :] = d_head[48 * p:48 * p + 48, :]


def attend_back_kernel(
    info, do_parts, qkv_hbm, inverse, w_t_hbm, hot_t_hbm, scales_hbm, dy_hbm, eh_hbm, el_hbm, xh_hbm, xl_hbm, slopes_hbm,
    sent,
    qkv_ref, w_t, hot_t, scales, dy, eh_all, el_all, xh, xl, slopes, do_all, g_t, dk_acc, dv_acc, d_x_all, conv_acc, dconv, sems, e_sems,
):
    half, m = info[0], info[1]
    steps = TOKENS // TILE
    e_copies = [
        [pltpu.make_async_copy(there.at[c], here.at[c], e_sems.at[i, c]) for i, (there, here) in enumerate(((eh_hbm, eh_all), (el_hbm, el_all)))]
        for c in range(steps)
    ]
    copies = [pltpu.make_async_copy(a, b, sems.at[i]) for i, (a, b) in enumerate(((dy_hbm, dy), (xh_hbm, xh), (xl_hbm, xl), (w_t_hbm, w_t), (hot_t_hbm, hot_t), (scales_hbm, scales)))]
    copies += [
        pltpu.make_async_copy(slopes_hbm.at[pl.ds(c * TILE, TILE)], slopes.at[pl.ds(c * TILE, TILE)], sems.at[6 + c]) for c in range(steps)
    ]
    qkv_copy = pltpu.make_async_copy(qkv_hbm, qkv_ref, sems.at[10])
    qkv_copy.start()
    for pair in e_copies:
        for copy in pair:
            copy.start()
    for copy in copies:
        copy.start()
    for p in range(GROUP):
        both = jnp.transpose(do_parts[p * OWN:(p + 1) * OWN, :])
        do_all[p * OWN:(p + 1) * OWN, :] = both[:OWN]
        do_all[512 + p * OWN:512 + (p + 1) * OWN, :] = both[OWN:]
    qkv_copy.wait()
    qkv = qkv_ref[...]
    kh, kl = split2(jnp.transpose(qkv[:, HS:2 * HS]))
    k_both = jnp.concatenate([kh, kl], axis=0)
    vh, vl = split2(qkv[:, 2 * HS:])
    v_three = jnp.concatenate([vh, vh, vl], axis=1)
    turned = jnp.transpose(do_all[...])
    dth, dtl = split2(turned)
    do_t = jnp.concatenate([dth, dtl, dth], axis=0)
    dh, dl = split2(jnp.transpose(turned * inverse[...]))
    do_both = jnp.concatenate([dh, dl], axis=1)
    qh, ql = split2(qkv[:, :HS])
    q_both = jnp.concatenate([qh, ql], axis=1)
    following = dot(v_three, do_t[:, :TILE])
    for c in range(steps):
        here = slice(c * TILE, (c + 1) * TILE)
        dp = following
        if c + 1 < steps:
            following = dot(v_three, do_t[:, (c + 1) * TILE:(c + 2) * TILE])
        for copy in e_copies[c]:
            copy.wait()
        eh, el = eh_all[c], el_all[c]
        p = (eh.astype(F32) + el.astype(F32)) * inverse[:, here]
        ds = p * (dp - jnp.sum(p * dp, axis=0, keepdims=True))
        sh, sl = split2(ds)
        both = dot(k_both, sh)
        g_t[0:HS, here] = (both[:HS] + (both[HS:] + dot(kh, sl))) * (HS ** -0.5)
        both = dot(eh, do_both[here])
        dv = both[:, :HS] + (both[:, HS:] + dot(el, dh[here]))
        both = dot(sh, q_both[here])
        dk = both[:, :HS] + (both[:, HS:] + dot(sl, qh[here]))
        if c == 0:
            dk_acc[...] = dk
            dv_acc[...] = dv
        else:
            dk_acc[...] += dk
            dv_acc[...] += dv
    g_t[HS:2 * HS, :] = jnp.transpose(dk_acc[...])
    g_t[2 * HS:3 * HS, :] = jnp.transpose(dv_acc[...])
    for copy in copies[:6]:
        copy.wait()
    lanes = pl.ds(pl.multiple_of(half * 384, 128), 384)
    gh, gl = split2(g_t[...])
    both = dot(jnp.concatenate([gh, gl], axis=0), xh[:, lanes])
    d_w = jnp.transpose(both[:192] + (both[192:] + dot(gh, xl[:, lanes])))

    wh, wl = split2(w_t[...])
    w_three = jnp.concatenate([wh, wl, wh], axis=0)

    def back_to_xn(c):
        gh, gl = split2(jnp.transpose(g_t[:, c * 512:(c + 1) * 512]))
        return dot(jnp.concatenate([gh, gh, gl], axis=1), w_three)

    own = pl.ds(pl.multiple_of(m * OWN, OWN), OWN)
    following = back_to_xn(0)
    for c in range(2):
        here = slice(c * 512, (c + 1) * 512)
        d_xn = following
        if c + 1 < 2:
            following = back_to_xn(c + 1)
        xn = xh[here].astype(F32) + xl[here].astype(F32)
        mean = jnp.mean(d_xn * xn, axis=-1, keepdims=True)
        d_x_all[...] = scales[here, :1] * (d_xn - xn * mean) * (0.5 / POOL)
        d_x_all[own, :] += dy[c * OWN:(c + 1) * OWN, :] * (0.5 / POOL)
        d_x = d_x_all[...]
        copies[6 + 2 * c].wait()
        copies[7 + 2 * c].wait()
        hot = hot_t[:, here]
        for r in range(POOL):
            dh, dl = split2(d_x * slopes[here, r * C:(r + 1) * C])
            moved = dot(hot, dh) + dot(hot, dl)
            if c == 0:
                conv_acc[r] = moved
            else:
                conv_acc[r] += moved
    summed = conv_acc[0, 4:4 + 4 * KW, :]
    for r in range(1, POOL):
        summed += conv_acc[r, 4 * (r + 1):4 * (r + 1) + 4 * KW, :]
    dconv[...] = jnp.zeros_like(dconv)
    dconv[0:4 * KW, :] = summed
    d_conv = jnp.transpose(dconv[:, lanes])
    for p in range(GROUP):
        mine = d_w[48 * p:48 * p + 48, :]
        sent[p, 0:48, :] = mine[:, :128]
        sent[p, 48:72, :] = jnp.concatenate([mine[:24, 128:], mine[24:, 128:]], axis=1)
        mine = d_conv[48 * p:48 * p + 48, :HS]
        sent[p, 72:96, :] = jnp.concatenate([mine[:24], mine[24:]], axis=1)


def sum_kernel(grads, d_out, d_head):
    every = grads[0]
    for p in range(1, GROUP):
        every = every + grads[p]
    d_out[...] = jnp.concatenate([every[32 * j:32 * j + 32, :] for j in range(6)], axis=1)
    d_head[...] = every[192:240, :]


def finish_kernel(got, d_conv, d_query, d_key, d_value):
    total = got[0, 72:96, :]
    for p in range(1, GROUP):
        total = total + got[p, 72:96, :]
    d_conv[...] = jnp.concatenate([total[:, :HS], total[:, HS:]], axis=0)[:, :4 * KW]
    for part, out in enumerate((d_query, d_key)):
        out[...] = jnp.concatenate([got[h, 0:48, part * HS:(part + 1) * HS] for h in range(HEADS)], axis=1)
    rows = [got[h, 48:72, :] for h in range(HEADS)]
    d_value[...] = jnp.concatenate([jnp.concatenate([r[:, :HS], r[:, HS:]], axis=0) for r in rows], axis=1)


def shape(*dims, dtype=F32):
    return jax.ShapeDtypeStruct(dims, dtype)


def params(mib=60):
    return pltpu.CompilerParams(vmem_limit_bytes=mib * 1024 * 1024)


def attend():
    return pl.pallas_call(
        attend_kernel,
        out_shape=(
            shape(2 * OWN, C), shape(128, TOKENS, dtype=BF16), shape(1, TOKENS), shape(512, 128),
            shape(TOKENS, C, dtype=BF16), shape(TOKENS, C, dtype=BF16), shape(TOKENS, 128), shape(TOKENS, 3 * HS), shape(3 * HS, C),
            shape(TOKENS, POOL * C), shape(4, TOKENS, TILE, dtype=BF16), shape(4, TOKENS, TILE, dtype=BF16),
        ),
        in_specs=[SMEM, VMEM, VMEM, ANY, ANY, ANY],
        out_specs=(VMEM,) * 4 + (ANY,) * 8,
        scratch_shapes=[
            pltpu.VMEM((POOL, WIN, C), F32),
            pltpu.VMEM((256, POOL * C), BF16),
            pltpu.VMEM((TOKENS + 16, 256), F32),
            pltpu.VMEM((3, C, 128), F32),
            pltpu.VMEM((TOKENS, C), F32),
            pltpu.VMEM((TOKENS, C), BF16),
            pltpu.VMEM((TOKENS, C), BF16),
            pltpu.VMEM((TOKENS, 128), F32),
            pltpu.VMEM((TOKENS, 3 * HS), F32),
            pltpu.VMEM((3 * HS, C), F32),
            pltpu.VMEM((TOKENS, POOL * C), F32),
            pltpu.VMEM((4, TOKENS, TILE), BF16),
            pltpu.VMEM((4, TOKENS, TILE), BF16),
            pltpu.SemaphoreType.DMA((3,)),
            pltpu.SemaphoreType.DMA((4,)),
            pltpu.SemaphoreType.DMA((2, 4)),
            pltpu.SemaphoreType.DMA((2,)),
            pltpu.SemaphoreType.DMA((3, 4)),
        ],
        compiler_params=params(),
        name="attend",
    )


def decode():
    return pl.pallas_call(
        decode_kernel,
        out_shape=(shape(OWN, TRACKS), shape(HD, 128), shape(2 * OWN, C), shape(2 * OWN, C), shape(2 * OWN, TRACKS)),
        in_specs=[VMEM] * 6,
        out_specs=(VMEM,) * 5,
        compiler_params=params(16),
        name="decode",
    )


def share():
    return pl.pallas_call(
        share_kernel,
        out_shape=shape(GROUP, 240, 128),
        in_specs=[SMEM] + [VMEM] * 4,
        out_specs=VMEM,
        compiler_params=params(16),
        name="share",
    )


def attend_back():
    return pl.pallas_call(
        attend_back_kernel,
        out_shape=shape(GROUP, 96, 128),
        in_specs=[SMEM, VMEM, ANY, VMEM] + [ANY] * 9,
        out_specs=VMEM,
        scratch_shapes=[
            pltpu.VMEM((TOKENS, 3 * HS), F32),
            pltpu.VMEM((3 * HS, C), F32),
            pltpu.VMEM((128, TOKENS), BF16),
            pltpu.VMEM((TOKENS, 128), F32),
            pltpu.VMEM((2 * OWN, C), F32),
            pltpu.VMEM((4, TOKENS, TILE), BF16),
            pltpu.VMEM((4, TOKENS, TILE), BF16),
            pltpu.VMEM((TOKENS, C), BF16),
            pltpu.VMEM((TOKENS, C), BF16),
            pltpu.VMEM((TOKENS, POOL * C), F32),
            pltpu.VMEM((TOKENS, HS), F32),
            pltpu.VMEM((3 * HS, TOKENS), F32),
            pltpu.VMEM((TOKENS, HS), F32),
            pltpu.VMEM((TOKENS, HS), F32),
            pltpu.VMEM((512, C), F32),
            pltpu.VMEM((POOL, 128, C), F32),
            pltpu.VMEM((128, C), F32),
            pltpu.SemaphoreType.DMA((11,)),
            pltpu.SemaphoreType.DMA((2, 4)),
        ],
        compiler_params=params(),
        name="attend_back",
    )


def add_up():
    return pl.pallas_call(
        sum_kernel,
        out_shape=(shape(32, C), shape(48, TRACKS)),
        in_specs=[VMEM],
        out_specs=(VMEM,) * 2,
        compiler_params=params(8),
        name="add_up",
    )


def finish():
    return pl.pallas_call(
        finish_kernel,
        out_shape=(shape(48, 4 * KW), shape(48, HD), shape(48, HD), shape(48, HD)),
        in_specs=[VMEM],
        out_specs=(VMEM,) * 4,
        compiler_params=params(8),
        name="finish",
    )


def per_device(bases, targets, w_conv, w_query, w_key, w_value, w_out, w_head):
    s = lax.axis_index("seq")
    info = jnp.stack([lax.div(s, GROUP), lax.rem(s, GROUP)]).astype(jnp.int32)
    groups = [list(range(GROUP)), list(range(GROUP, 2 * GROUP))]

    def exchange(value):
        return lax.all_to_all(value, "seq", 0, 0, axis_index_groups=groups, tiled=True)

    targets_there = lax.ppermute(targets, "seq", [(i, i ^ GROUP) for i in range(2 * GROUP)])
    every = lax.all_to_all(jnp.broadcast_to(bases.reshape(1, 2, 128), (16, 2, 128)), "seq", 0, 0, tiled=True)

    every, targets_there = lax.optimization_barrier((every, targets_there))
    x_own, hot_t, inverse, o_here, xh, xl, scales, qkv, w_t, slopes, eh, el = attend()(info, every, w_conv, w_query, w_key, w_value)
    o_parts = exchange(o_here)
    log_rate, do_sent, dy, yn, d_rate = decode()(o_parts, x_own, targets, targets_there, w_out, w_head)
    do_parts = exchange(do_sent)
    grads = exchange(share()(info, o_parts, dy, yn, d_rate))
    sent = attend_back()(info, do_parts, qkv, inverse, w_t, hot_t, scales, dy, eh, el, xh, xl, slopes)
    sent, grads = lax.optimization_barrier((sent, grads))
    d_out, d_head = add_up()(grads)
    d_conv, d_query, d_key, d_value = finish()(exchange(sent))
    return (log_rate, jnp.transpose(d_conv), d_query, d_key, d_value, d_out, d_head)


def solution(mesh):
    rows = P(("dp", "seq"), None)
    return jax.shard_map(
        per_device,
        mesh=mesh,
        in_specs=(P(("dp", "seq")), rows, P(), P(), P(), P(), P(), P()),
        out_specs=(rows, P("dp", "seq"), rows, rows, rows, rows, rows),
        check_vma=False,
    )
```

```python
import math

import jax
import jax.numpy as jnp
from jax import lax
from jax.experimental import pallas as pl
from jax.experimental.pallas import tpu as pltpu
from jax.sharding import PartitionSpec as P


C = 768
KW = 15
HEADS = 8
HS = 64
TRACKS = 128
POOL = 4
HD = 512
TOKENS = 1024
GROUP = 8
OWN = 64
F32 = jnp.float32
BF16 = jnp.bfloat16
GELU_A = math.sqrt(2.0 / math.pi)
GELU_C = 0.044715 / GELU_A ** 2
WIN = 80
TILE = 256

VMEM = pl.BlockSpec(memory_space=pltpu.VMEM)
SMEM = pl.BlockSpec(memory_space=pltpu.SMEM)
ANY = pl.BlockSpec(memory_space=pl.ANY)


def dot(left, right):
    return lax.dot_general(left, right, (((1,), (0,)), ((), ())), preferred_element_type=F32)


def split2(a):
    hi = a.astype(BF16)
    return hi, (a - hi.astype(F32)).astype(BF16)


def split3(a):
    hi = a.astype(BF16)
    rest = a - hi.astype(F32)
    mid = rest.astype(BF16)
    return hi, mid, (rest - mid.astype(F32)).astype(BF16)


def dot3(left, right):
    lh, ll = split2(left)
    rh, rl = split2(right)
    return dot(lh, rh) + (dot(lh, rl) + dot(ll, rh))


def dot3_narrow(left, right):
    lh, ll = split2(left)
    rh, rl = split2(right)
    n = right.shape[1]
    both = dot(lh, jnp.concatenate([rh, rl], axis=1))
    return both[:, :n] + (both[:, n:] + dot(ll, rh))


def dot3_short(left, right):
    lh, ll = split2(left)
    rh, rl = split2(right)
    n = left.shape[0]
    both = dot(jnp.concatenate([lh, ll], axis=0), rh)
    return both[:n] + (both[n:] + dot(lh, rl))


def dot3_thin(left, right):
    lh, ll = split2(left)
    rh, rl = split2(right)
    return dot(jnp.concatenate([lh, lh, ll], axis=1), jnp.concatenate([rh, rl, rh], axis=0))


def dot6(left, right):
    lh, lm, ll = split3(left)
    rh, rm, rl = split3(right)
    return dot(lh, rh) + ((dot(lh, rm) + dot(lm, rh)) + (dot(lm, rm) + (dot(lh, rl) + dot(ll, rh))))


def rms_scale(a):
    return lax.rsqrt(jnp.mean(a * a, axis=-1, keepdims=True) + 1e-06)


def conv_weights(w_ref, pad_ref, out_ref):
    pad_ref[...] = jnp.zeros_like(pad_ref)
    for r in range(POOL):
        pad_ref[r, 4 * (r + 1):4 * (r + 1) + 4 * KW, :] = w_ref[...] * GELU_A
    for r in range(POOL):
        pieces = split3(pad_ref[r])
        zeros = jnp.zeros((256 - 3 * WIN, C), BF16)
        out_ref[:, r * C:(r + 1) * C] = jnp.concatenate([*pieces, zeros], axis=0)


def key_stack(k):
    h, m, l = split3(k)
    return h, jnp.concatenate([m, l, h, m, h], axis=1)


def query_stack(q_t):
    h, m, l = split3(q_t)
    return h, jnp.concatenate([h, h, m, m, l], axis=0)


def attend_kernel(
    info, bases, w_conv, wq_hbm, wk_hbm, wv_hbm,
    x_own, hot_t, inverse, o_out, xh_hbm, xl_hbm, scale_hbm, qkv_hbm, w_t_hbm, slopes_hbm, eh_hbm, el_hbm,
    pad, w_all, window, slabs, x_all, xh_out, xl_out, scale_out, qkv_out, w_t, slopes, eh_all, el_all, sems, slope_sems, e_sems, out_sems, chunk_sems,
):
    half, m = info[0], info[1]
    copies = []
    for i, w in enumerate((wq_hbm, wk_hbm, wv_hbm)):
        lanes = pl.ds(pl.multiple_of(lax.div(m, 2) * 128, 128), 128)
        copies.append(pltpu.make_async_copy(w.at[:, lanes], slabs.at[i], sems.at[i]))
    for copy in copies:
        copy.start()
    conv_weights(w_conv, pad, w_all)

    lane = lax.broadcasted_iota(jnp.int32, (128, 256), 1)
    row = lax.broadcasted_iota(jnp.int32, (128, 256), 0)
    within = lax.rem(lane, WIN)
    place = lax.div(lax.rem(within, 16), 4)
    pick = jnp.where(lax.rem(row, 4) == place, 1.0, 0.0).astype(BF16)
    mine = lax.broadcasted_iota(jnp.int32, (32, 128), 0) == lax.div(lax.broadcasted_iota(jnp.int32, (32, 128), 1), 4)
    code = lax.rem(lax.broadcasted_iota(jnp.int32, (1, 256), 1), 4).astype(F32)
    window[0:8, :] = jnp.zeros((8, 256), F32)
    window[TOKENS + 8:TOKENS + 16, :] = jnp.zeros((8, 256), F32)
    for part in range(8):
        pieces = []
        for q in range(4 * part, 4 * part + 4):
            line = bases[q // 2, q % 2:q % 2 + 1, :].astype(F32)
            pieces.append(jnp.where(mine, jnp.broadcast_to(line, (32, 128)), 0.0))
        value = dot(jnp.concatenate(pieces, axis=0).astype(BF16), pick)
        window[8 + 128 * part:8 + 128 * part + 128, :] = jnp.where(value == code, 1.0, 0.0)

    shift = lax.div(lax.rem(lax.broadcasted_iota(jnp.int32, (TILE, 256), 1), WIN), 16)
    real = lax.broadcasted_iota(jnp.int32, (TILE, 256), 1) < 3 * WIN
    steps = TOKENS // TILE

    def encode(c, _):
        start = pl.multiple_of(lax.rem(c + half * (steps // 2), steps) * TILE, TILE)
        around = window[pl.ds(start, TILE + 16), :]
        hot = jnp.zeros((TILE, 256), F32)
        for d in range(5):
            hot = jnp.where(shift == d, around[6 + d:6 + d + TILE, :], hot)
        hot = jnp.where(real, hot, 0.0).astype(BF16)
        here = pl.ds(pl.multiple_of(c * TILE, TILE), TILE)
        total = None
        for r in range(POOL):
            y = dot(hot, w_all[:, r * C:(r + 1) * C])
            cube = y * (y * y * GELU_C)
            t = jnp.tanh(y + cube)
            up = 1.0 + t
            total = y * up if total is None else total + y * up
            slopes[here, r * C:(r + 1) * C] = up + (1.0 - t * t) * (y + 3.0 * cube)
        x_all[here, :] = total * (0.5 / (GELU_A * POOL))
        hot_t[:, here] = jnp.transpose(hot[:, :128].astype(F32)).astype(BF16)
        pltpu.make_async_copy(slopes.at[here], slopes_hbm.at[here], slope_sems.at[c]).start()
        return 0

    for copy in copies:
        copy.wait()
    odd = lax.rem(m, 2) == 1
    columns = [jnp.where(odd, slabs[i, :, HS:], slabs[i, :, :HS]) for i in range(3)]
    w_t[...] = jnp.transpose(jnp.concatenate(columns, axis=1))
    w_qkv = jnp.concatenate([columns[0] * HS ** -0.5, columns[1], columns[2]], axis=1)
    wh, wm, wl = split3(w_qkv)

    chunked = ((xh_out, xh_hbm), (xl_out, xl_hbm), (scale_out, scale_hbm))

    def project(c, _):
        here = pl.ds(pl.multiple_of(c * TILE, TILE), TILE)
        x = x_all[here, :]
        scale = rms_scale(x)
        scale_out[here, :] = jnp.broadcast_to(scale, (TILE, 128))
        xn = x * scale
        h, mid, low = split3(xn)
        xh_out[here, :] = h
        xl_out[here, :] = mid
        for i, (a, b) in enumerate(chunked):
            pltpu.make_async_copy(a.at[here], b.at[here], chunk_sems.at[i, c]).start()
        qkv_out[here, :] = dot(h, wh) + ((dot(h, wm) + dot(mid, wh)) + (dot(mid, wm) + (dot(h, wl) + dot(low, wh))))
        return 0

    encode(0, 0)

    def both_steps(c, _):
        project(c - 1, 0)
        encode(c, 0)
        return 0

    lax.fori_loop(1, steps, both_steps, 0)
    project(steps - 1, 0)
    for part in range(2):
        here = pl.ds(pl.multiple_of(part * 512 + m * OWN, OWN), OWN)
        x_own[part * OWN:(part + 1) * OWN, :] = x_all[here, :]

    outs_copies = [
        pltpu.make_async_copy(a, b, out_sems.at[i])
        for i, (a, b) in enumerate(((qkv_out, qkv_hbm), (w_t, w_t_hbm)))
    ]
    for copy in outs_copies:
        copy.start()
    qkv = qkv_out[...]
    q_t = query_stack(jnp.transpose(qkv[:, :HS]))
    keys = key_stack(qkv[:, HS:2 * HS])
    vh, vl = split2(jnp.transpose(qkv[:, 2 * HS:]))
    v_both = jnp.concatenate([vh, vl], axis=0)
    outs = []

    def scores_of(c):
        there = slice(c * TILE, (c + 1) * TILE)
        return dot(keys[0], q_t[0][:, there]) + dot(keys[1], q_t[1][:, there])

    following = scores_of(0)
    for c in range(steps):
        scores = following
        if c + 1 < steps:
            following = scores_of(c + 1)
        e = jnp.exp(scores - jnp.max(scores, axis=0, keepdims=True))
        eh, el = split2(e)
        over = 1.0 / jnp.sum(eh.astype(F32) + el.astype(F32), axis=0, keepdims=True)
        inverse[:, c * TILE:(c + 1) * TILE] = over
        eh_all[c] = eh
        el_all[c] = el
        for i, (here, there) in enumerate(((eh_all, eh_hbm), (el_all, el_hbm))):
            pltpu.make_async_copy(here.at[c], there.at[c], e_sems.at[i, c]).start()
        both = dot(v_both, eh)
        outs.append(jnp.transpose((both[:HS] + (both[HS:] + dot(vh, el))) * over))
    o_out[...] = jnp.concatenate(
        [jnp.concatenate(outs[:steps // 2], axis=0), jnp.concatenate(outs[steps // 2:], axis=0)], axis=1
    )
    for copy in outs_copies:
        copy.wait()
    for c in range(steps):
        here = pl.ds(c * TILE, TILE)
        for i, (a, b) in enumerate(chunked):
            pltpu.make_async_copy(a.at[here], b.at[here], chunk_sems.at[i, c]).wait()
        pltpu.make_async_copy(slopes.at[here], slopes_hbm.at[here], slope_sems.at[c]).wait()
        pltpu.make_async_copy(eh_all.at[c], eh_hbm.at[c], e_sems.at[0, c]).wait()
        pltpu.make_async_copy(el_all.at[c], el_hbm.at[c], e_sems.at[1, c]).wait()


def decode_kernel(
    o_parts, x_own, targets_here, targets_there, w_out, w_head,
    log_rate, do_out, dy_out, yn_all, d_rate_out,
):
    parts = [o_parts[h * OWN:(h + 1) * OWN, :] for h in range(HEADS)]
    attended = jnp.concatenate(
        [jnp.concatenate([p[:, :HS] for p in parts], axis=1), jnp.concatenate([p[:, HS:] for p in parts], axis=1)], axis=0
    )
    wout = w_out[...]
    wouth, woutl = split2(wout)
    ah, al = split2(attended)
    both = dot(jnp.concatenate([ah, al], axis=0), wouth)
    y = x_own[...] + (both[:2 * OWN] + (both[2 * OWN:] + dot(ah, woutl)))
    scale = rms_scale(y)
    yn = y * scale
    yn_all[...] = yn
    rate = dot3_narrow(yn, w_head[...])
    log_rate[...] = rate[:OWN]
    targets = jnp.concatenate([targets_here[...], targets_there[...]], axis=0).astype(F32)
    d_rate = (jnp.exp(rate) - targets) * (1.0 / math.sqrt(TOKENS))
    d_rate_out[...] = d_rate
    d_yn = dot3_thin(d_rate, jnp.transpose(w_head[...]))
    dy = scale * (d_yn - yn * jnp.mean(d_yn * yn, axis=-1, keepdims=True))
    dy_out[...] = dy
    dth, dtl = split2(jnp.transpose(dy))
    both = dot(wouth, jnp.concatenate([dth, dtl], axis=1))
    do_out[...] = both[:, :2 * OWN] + (both[:, 2 * OWN:] + dot(woutl, dth))


def share_kernel(info, o_parts, dy, yn_all, d_rate_ref, grads_out):
    half = info[0]
    d_rate = d_rate_ref[...]
    heads = o_parts[pl.ds(pl.multiple_of(half * 256, 256), 256), :]
    o_t = jnp.concatenate(
        [
            jnp.concatenate(
                [jnp.transpose(heads[h * OWN:(h + 1) * OWN, :])[:HS], jnp.transpose(heads[h * OWN:(h + 1) * OWN, :])[HS:]], axis=1
            )
            for h in range(4)
        ],
        axis=0,
    )
    d_out = dot3_thin(o_t, dy[...])
    yn_half = yn_all[:, pl.ds(pl.multiple_of(half * 384, 128), 384)]
    d_head = dot3_thin(jnp.transpose(yn_half), d_rate)
    for p in range(GROUP):
        for j in range(6):
            grads_out[p, 32 * j:32 * j + 32, :] = d_out[32 * p:32 * p + 32, 128 * j:128 * j + 128]
        grads_out[p, 192:240, :] = d_head[48 * p:48 * p + 48, :]


def attend_back_kernel(
    info, do_parts, qkv_hbm, inverse, w_t_hbm, hot_t_hbm, scales_hbm, dy_hbm, eh_hbm, el_hbm, xh_hbm, xl_hbm, slopes_hbm,
    sent,
    qkv_ref, w_t, hot_t, scales, dy, eh_all, el_all, xh, xl, slopes, do_all, g_t, dk_acc, dv_acc, d_x_all, conv_acc, dconv, sems, e_sems,
):
    half, m = info[0], info[1]
    steps = TOKENS // TILE
    e_copies = [
        [pltpu.make_async_copy(there.at[c], here.at[c], e_sems.at[i, c]) for i, (there, here) in enumerate(((eh_hbm, eh_all), (el_hbm, el_all)))]
        for c in range(steps)
    ]
    copies = [pltpu.make_async_copy(a, b, sems.at[i]) for i, (a, b) in enumerate(((dy_hbm, dy), (xh_hbm, xh), (xl_hbm, xl), (w_t_hbm, w_t), (hot_t_hbm, hot_t), (scales_hbm, scales)))]
    copies += [
        pltpu.make_async_copy(slopes_hbm.at[pl.ds(c * TILE, TILE)], slopes.at[pl.ds(c * TILE, TILE)], sems.at[6 + c]) for c in range(steps)
    ]
    qkv_copy = pltpu.make_async_copy(qkv_hbm, qkv_ref, sems.at[10])
    qkv_copy.start()
    for pair in e_copies:
        for copy in pair:
            copy.start()
    for copy in copies:
        copy.start()
    for p in range(GROUP):
        both = jnp.transpose(do_parts[p * OWN:(p + 1) * OWN, :])
        do_all[p * OWN:(p + 1) * OWN, :] = both[:OWN]
        do_all[512 + p * OWN:512 + (p + 1) * OWN, :] = both[OWN:]
    qkv_copy.wait()
    qkv = qkv_ref[...]
    kh, kl = split2(jnp.transpose(qkv[:, HS:2 * HS]))
    k_both = jnp.concatenate([kh, kl], axis=0)
    vh, vl = split2(qkv[:, 2 * HS:])
    v_three = jnp.concatenate([vh, vh, vl], axis=1)
    turned = jnp.transpose(do_all[...])
    dth, dtl = split2(turned)
    do_t = jnp.concatenate([dth, dtl, dth], axis=0)
    dh, dl = split2(jnp.transpose(turned * inverse[...]))
    do_both = jnp.concatenate([dh, dl], axis=1)
    qh, ql = split2(qkv[:, :HS])
    q_both = jnp.concatenate([qh, ql], axis=1)
    following = dot(v_three, do_t[:, :TILE])
    for c in range(steps):
        here = slice(c * TILE, (c + 1) * TILE)
        dp = following
        if c + 1 < steps:
            following = dot(v_three, do_t[:, (c + 1) * TILE:(c + 2) * TILE])
        for copy in e_copies[c]:
            copy.wait()
        eh, el = eh_all[c], el_all[c]
        p = (eh.astype(F32) + el.astype(F32)) * inverse[:, here]
        ds = p * (dp - jnp.sum(p * dp, axis=0, keepdims=True))
        sh, sl = split2(ds)
        both = dot(k_both, sh)
        g_t[0:HS, here] = (both[:HS] + (both[HS:] + dot(kh, sl))) * (HS ** -0.5)
        both = dot(eh, do_both[here])
        dv = both[:, :HS] + (both[:, HS:] + dot(el, dh[here]))
        both = dot(sh, q_both[here])
        dk = both[:, :HS] + (both[:, HS:] + dot(sl, qh[here]))
        if c == 0:
            dk_acc[...] = dk
            dv_acc[...] = dv
        else:
            dk_acc[...] += dk
            dv_acc[...] += dv
    g_t[HS:2 * HS, :] = jnp.transpose(dk_acc[...])
    g_t[2 * HS:3 * HS, :] = jnp.transpose(dv_acc[...])
    for copy in copies[:6]:
        copy.wait()
    lanes = pl.ds(pl.multiple_of(half * 384, 128), 384)
    gh, gl = split2(g_t[...])
    both = dot(jnp.concatenate([gh, gl], axis=0), xh[:, lanes])
    d_w = jnp.transpose(both[:192] + (both[192:] + dot(gh, xl[:, lanes])))

    wh, wl = split2(w_t[...])
    w_three = jnp.concatenate([wh, wl, wh], axis=0)

    def back_to_xn(c):
        gh, gl = split2(jnp.transpose(g_t[:, c * 512:(c + 1) * 512]))
        return dot(jnp.concatenate([gh, gh, gl], axis=1), w_three)

    own = pl.ds(pl.multiple_of(m * OWN, OWN), OWN)
    following = back_to_xn(0)
    for c in range(2):
        here = slice(c * 512, (c + 1) * 512)
        d_xn = following
        if c + 1 < 2:
            following = back_to_xn(c + 1)
        xn = xh[here].astype(F32) + xl[here].astype(F32)
        mean = jnp.mean(d_xn * xn, axis=-1, keepdims=True)
        d_x_all[...] = scales[here, :1] * (d_xn - xn * mean) * (0.5 / POOL)
        d_x_all[own, :] += dy[c * OWN:(c + 1) * OWN, :] * (0.5 / POOL)
        d_x = d_x_all[...]
        copies[6 + 2 * c].wait()
        copies[7 + 2 * c].wait()
        hot = hot_t[:, here]
        for r in range(POOL):
            dh, dl = split2(d_x * slopes[here, r * C:(r + 1) * C])
            moved = dot(hot, dh) + dot(hot, dl)
            if c == 0:
                conv_acc[r] = moved
            else:
                conv_acc[r] += moved
    summed = conv_acc[0, 4:4 + 4 * KW, :]
    for r in range(1, POOL):
        summed += conv_acc[r, 4 * (r + 1):4 * (r + 1) + 4 * KW, :]
    dconv[...] = jnp.zeros_like(dconv)
    dconv[0:4 * KW, :] = summed
    d_conv = jnp.transpose(dconv[:, lanes])
    for p in range(GROUP):
        mine = d_w[48 * p:48 * p + 48, :]
        sent[p, 0:48, :] = mine[:, :128]
        sent[p, 48:72, :] = jnp.concatenate([mine[:24, 128:], mine[24:, 128:]], axis=1)
        mine = d_conv[48 * p:48 * p + 48, :HS]
        sent[p, 72:96, :] = jnp.concatenate([mine[:24], mine[24:]], axis=1)


def sum_kernel(grads, d_out, d_head):
    every = grads[0]
    for p in range(1, GROUP):
        every = every + grads[p]
    d_out[...] = jnp.concatenate([every[32 * j:32 * j + 32, :] for j in range(6)], axis=1)
    d_head[...] = every[192:240, :]


def finish_kernel(got, d_conv, d_query, d_key, d_value):
    total = got[0, 72:96, :]
    for p in range(1, GROUP):
        total = total + got[p, 72:96, :]
    d_conv[...] = jnp.concatenate([total[:, :HS], total[:, HS:]], axis=0)[:, :4 * KW]
    for part, out in enumerate((d_query, d_key)):
        out[...] = jnp.concatenate([got[h, 0:48, part * HS:(part + 1) * HS] for h in range(HEADS)], axis=1)
    rows = [got[h, 48:72, :] for h in range(HEADS)]
    d_value[...] = jnp.concatenate([jnp.concatenate([r[:, :HS], r[:, HS:]], axis=0) for r in rows], axis=1)


def shape(*dims, dtype=F32):
    return jax.ShapeDtypeStruct(dims, dtype)


def params(mib=60):
    return pltpu.CompilerParams(vmem_limit_bytes=mib * 1024 * 1024)


def attend():
    return pl.pallas_call(
        attend_kernel,
        out_shape=(
            shape(2 * OWN, C), shape(128, TOKENS, dtype=BF16), shape(1, TOKENS), shape(512, 128),
            shape(TOKENS, C, dtype=BF16), shape(TOKENS, C, dtype=BF16), shape(TOKENS, 128), shape(TOKENS, 3 * HS), shape(3 * HS, C),
            shape(TOKENS, POOL * C), shape(4, TOKENS, TILE, dtype=BF16), shape(4, TOKENS, TILE, dtype=BF16),
        ),
        in_specs=[SMEM, VMEM, VMEM, ANY, ANY, ANY],
        out_specs=(VMEM,) * 4 + (ANY,) * 8,
        scratch_shapes=[
            pltpu.VMEM((POOL, WIN, C), F32),
            pltpu.VMEM((256, POOL * C), BF16),
            pltpu.VMEM((TOKENS + 16, 256), F32),
            pltpu.VMEM((3, C, 128), F32),
            pltpu.VMEM((TOKENS, C), F32),
            pltpu.VMEM((TOKENS, C), BF16),
            pltpu.VMEM((TOKENS, C), BF16),
            pltpu.VMEM((TOKENS, 128), F32),
            pltpu.VMEM((TOKENS, 3 * HS), F32),
            pltpu.VMEM((3 * HS, C), F32),
            pltpu.VMEM((TOKENS, POOL * C), F32),
            pltpu.VMEM((4, TOKENS, TILE), BF16),
            pltpu.VMEM((4, TOKENS, TILE), BF16),
            pltpu.SemaphoreType.DMA((3,)),
            pltpu.SemaphoreType.DMA((4,)),
            pltpu.SemaphoreType.DMA((2, 4)),
            pltpu.SemaphoreType.DMA((2,)),
            pltpu.SemaphoreType.DMA((3, 4)),
        ],
        compiler_params=params(),
        name="attend",
    )


def decode():
    return pl.pallas_call(
        decode_kernel,
        out_shape=(shape(OWN, TRACKS), shape(HD, 128), shape(2 * OWN, C), shape(2 * OWN, C), shape(2 * OWN, TRACKS)),
        in_specs=[VMEM] * 6,
        out_specs=(VMEM,) * 5,
        compiler_params=params(16),
        name="decode",
    )


def share():
    return pl.pallas_call(
        share_kernel,
        out_shape=shape(GROUP, 240, 128),
        in_specs=[SMEM] + [VMEM] * 4,
        out_specs=VMEM,
        compiler_params=params(16),
        name="share",
    )


def attend_back():
    return pl.pallas_call(
        attend_back_kernel,
        out_shape=shape(GROUP, 96, 128),
        in_specs=[SMEM, VMEM, ANY, VMEM] + [ANY] * 9,
        out_specs=VMEM,
        scratch_shapes=[
            pltpu.VMEM((TOKENS, 3 * HS), F32),
            pltpu.VMEM((3 * HS, C), F32),
            pltpu.VMEM((128, TOKENS), BF16),
            pltpu.VMEM((TOKENS, 128), F32),
            pltpu.VMEM((2 * OWN, C), F32),
            pltpu.VMEM((4, TOKENS, TILE), BF16),
            pltpu.VMEM((4, TOKENS, TILE), BF16),
            pltpu.VMEM((TOKENS, C), BF16),
            pltpu.VMEM((TOKENS, C), BF16),
            pltpu.VMEM((TOKENS, POOL * C), F32),
            pltpu.VMEM((TOKENS, HS), F32),
            pltpu.VMEM((3 * HS, TOKENS), F32),
            pltpu.VMEM((TOKENS, HS), F32),
            pltpu.VMEM((TOKENS, HS), F32),
            pltpu.VMEM((512, C), F32),
            pltpu.VMEM((POOL, 128, C), F32),
            pltpu.VMEM((128, C), F32),
            pltpu.SemaphoreType.DMA((11,)),
            pltpu.SemaphoreType.DMA((2, 4)),
        ],
        compiler_params=params(),
        name="attend_back",
    )


def add_up():
    return pl.pallas_call(
        sum_kernel,
        out_shape=(shape(32, C), shape(48, TRACKS)),
        in_specs=[VMEM],
        out_specs=(VMEM,) * 2,
        compiler_params=params(8),
        name="add_up",
    )


def finish():
    return pl.pallas_call(
        finish_kernel,
        out_shape=(shape(48, 4 * KW), shape(48, HD), shape(48, HD), shape(48, HD)),
        in_specs=[VMEM],
        out_specs=(VMEM,) * 4,
        compiler_params=params(8),
        name="finish",
    )


def per_device(bases, targets, w_conv, w_query, w_key, w_value, w_out, w_head):
    s = lax.axis_index("seq")
    info = jnp.stack([lax.div(s, GROUP), lax.rem(s, GROUP)]).astype(jnp.int32)
    groups = [list(range(GROUP)), list(range(GROUP, 2 * GROUP))]

    def exchange(value):
        return lax.all_to_all(value, "seq", 0, 0, axis_index_groups=groups, tiled=True)

    targets_there = lax.ppermute(targets, "seq", [(i, i ^ GROUP) for i in range(2 * GROUP)])
    every = lax.all_to_all(jnp.broadcast_to(bases.reshape(1, 2, 128), (16, 2, 128)), "seq", 0, 0, tiled=True)

    every, targets_there = lax.optimization_barrier((every, targets_there))
    x_own, hot_t, inverse, o_here, xh, xl, scales, qkv, w_t, slopes, eh, el = attend()(info, every, w_conv, w_query, w_key, w_value)
    o_parts = exchange(o_here)
    log_rate, do_sent, dy, yn, d_rate = decode()(o_parts, x_own, targets, targets_there, w_out, w_head)
    do_parts = exchange(do_sent)
    grads = exchange(share()(info, o_parts, dy, yn, d_rate))
    sent = attend_back()(info, do_parts, qkv, inverse, w_t, hot_t, scales, dy, eh, el, xh, xl, slopes)
    sent, grads = lax.optimization_barrier((sent, grads))
    d_out, d_head = add_up()(grads)
    d_conv, d_query, d_key, d_value = finish()(exchange(sent))
    return (log_rate, jnp.transpose(d_conv), d_query, d_key, d_value, d_out, d_head)


def solution(mesh):
    rows = P(("dp", "seq"), None)
    return jax.shard_map(
        per_device,
        mesh=mesh,
        in_specs=(P(("dp", "seq")), rows, P(), P(), P(), P(), P(), P()),
        out_specs=(rows, P("dp", "seq"), rows, rows, rows, rows, rows),
        check_vma=False,
    )
```
